256 devices in a mesh: row: 32 (over x, y, core), col: 8 (over z).
Axes of the slice: x: 4, y: 4, z: 8, core: 2. Of those that a mesh axis runs over, the one named last changes fastest.
Arguments:
- a_stored: bfloat16 [24576, 24576], P('row', 'col'), may hold values from -6 to 6
- pivots: int32 [2, 256], replicated, may hold values from 0 to 24575, as said below
- l_inverse: bfloat16 [2, 256, 256], replicated, as said below
- u_inverse: bfloat16 [2, 256, 256], replicated, as said below
Outputs:
- a_factored: bfloat16 [24576, 24576], P('row', 'col')
The draws below stay inside these ranges and needn't reach their ends.
Inputs may be any that keep to these rules, and one draw needn't show every extreme that they name: `pivots`: for panel k, entry j is either k * 256 + j or a row at or after (k + 1) * 256; the entries of one panel are distinct; entry 0 of panel 0 is 0, entry 1 of panel k is global row (2) * 256 * 32 + ((k + 32 / 2) mod 32) * 256 + 256 / 2, and the last entry of each panel is 24575. `l_inverse`: lower triangular with unit diagonal. `u_inverse`: upper triangular with a positive diagonal.
All inputs are finite; a program needn't handle non-finite values.
Results may differ from the reference program's by a relative error of at most 0.0069.
Values may be sent and summed in bfloat16 or wider, within the bound.
A program may use at most 64 MiB of HBM per device.

```python
import jax
import jax.numpy as jnp

NB = 256
RB = 3
M = 24576
N_ROW = 32
N_COL = 8


def draw_pivots(key, part):
    key = jax.random.fold_in(key, 11)
    panels = []
    for section in range(2):
        sub_key = jax.random.fold_in(key, section)
        perm_key, keep_key = jax.random.split(sub_key)
        start_row = (section + 1) * NB
        forced_row = (RB - 1) * NB * N_ROW + (section + N_ROW // 2) % N_ROW * NB + NB // 2
        candidates = jax.random.permutation(perm_key, M - 2 - start_row)[:NB].astype(jnp.int32) + start_row
        candidates = candidates + (candidates >= forced_row).astype(jnp.int32)
        keeping = jax.random.randint(keep_key, (NB,), 0, 4) == 0
        own_rows = section * NB + jnp.arange(NB, dtype=jnp.int32)
        chosen = jnp.where(keeping, own_rows, candidates)
        chosen = chosen.at[1].set(forced_row)
        chosen = chosen.at[NB - 1].set(M - 1)
        if section == 0:
            chosen = chosen.at[0].set(0)
        panels.append(chosen)
    return jnp.stack(panels).astype(jnp.int32)


def draw_l_inverse(key, part):
    key = jax.random.fold_in(key, 21)
    noise = jax.random.normal(key, (2, NB, NB), jnp.float32)
    index = jnp.arange(NB)
    lower = index[:, None] > index[None, :]
    values = jnp.where(lower[None], noise * (0.5 / NB ** 0.5), 0.0) + jnp.eye(NB, dtype=jnp.float32)[None]
    return values.astype(jnp.bfloat16)


def draw_u_inverse(key, part):
    key = jax.random.fold_in(key, 31)
    noise_key, diag_key = jax.random.split(key)
    noise = jax.random.normal(noise_key, (2, NB, NB), jnp.float32)
    diagonal = jnp.exp(jax.random.uniform(diag_key, (2, NB), jnp.float32, -0.7, 0.0)) / NB ** 0.5
    index = jnp.arange(NB)
    upper = index[:, None] < index[None, :]
    eye_mask = (index[:, None] == index[None, :]).astype(jnp.float32)
    values = jnp.where(upper[None], noise * (0.5 / NB), 0.0) + eye_mask[None] * diagonal[:, None, :]
    return values.astype(jnp.bfloat16)


def level_of(own_key, extent, shards, least, largest):
    def one(axis_at, shards_of):
        draws = jax.random.uniform(jax.random.fold_in(jax.random.fold_in(own_key, 6), axis_at), (shards_of,), jnp.float32, least / len(shards), largest / len(shards))
        return jnp.repeat(jnp.exp(draws), extent[axis_at] // shards_of).reshape((-1,) + (1,) * (len(extent) - axis_at - 1))

    level = one(*shards[0])
    for cut in shards[1:]:
        level = level * one(*cut)
    return level


def centred(rng, dims, spread, most, cuts=(), kind=jnp.bfloat16):
    drawn = spread * jax.random.normal(rng, dims, jnp.float32)
    if cuts:
        drawn = drawn * level_of(rng, dims, cuts, -0.22, 0.18)
    return jnp.clip(drawn, -most, most).astype(kind)


def setup_inputs(seed: int = 0) -> dict:
    key_list = jax.random.split(jax.random.key(seed), 5)
    return {
        "a_stored": centred(key_list[0], (M, M), 1.0, 6.0, ((0, 32), (1, 8))),
        "pivots": draw_pivots(jax.random.fold_in(key_list[4], 71), 0),
        "l_inverse": draw_l_inverse(jax.random.fold_in(key_list[4], 71), 0),
        "u_inverse": draw_u_inverse(jax.random.fold_in(key_list[4], 71), 0),
    }


def to_global(stored):
    col_blocks = M // (NB * N_COL)
    shaped = stored.reshape(N_ROW, RB, NB, N_COL, col_blocks, NB)
    return shaped.transpose(1, 0, 2, 4, 3, 5).reshape(M, M)


def to_stored(matrix):
    col_blocks = M // (NB * N_COL)
    shaped = matrix.reshape(RB, N_ROW, NB, col_blocks, N_COL, NB)
    return shaped.transpose(1, 0, 2, 4, 3, 5).reshape(M, M)


def reference(a_stored, pivots, l_inverse, u_inverse):
    matrix = to_global(a_stored)
    for section in range(2):
        start_row = section * NB
        end_row = start_row + NB
        pivot_rows = pivots[section]
        top_rows = matrix[start_row:end_row]
        far_rows = matrix[pivot_rows]
        matrix = matrix.at[pivot_rows].set(top_rows)
        matrix = matrix.at[start_row:end_row].set(far_rows)
        lower_part = jnp.dot(matrix[end_row:, start_row:end_row], u_inverse[section], preferred_element_type=jnp.float32).astype(jnp.bfloat16)
        upper_part = jnp.dot(l_inverse[section], matrix[start_row:end_row, end_row:], preferred_element_type=jnp.float32).astype(jnp.bfloat16)
        matrix = matrix.at[end_row:, start_row:end_row].set(lower_part)
        matrix = matrix.at[start_row:end_row, end_row:].set(upper_part)
        pieces = []
        step_rows = 2048
        for first_row in range(end_row, M, step_rows):
            last_row = min(first_row + step_rows, M)
            block_rows = matrix[first_row:last_row, end_row:].astype(jnp.float32)
            product = jnp.dot(lower_part[first_row - end_row:last_row - end_row], upper_part, preferred_element_type=jnp.float32)
            pieces.append((block_rows - product).astype(jnp.bfloat16))
        matrix = matrix.at[end_row:, end_row:].set(jnp.concatenate(pieces, axis=0))
    return to_stored(matrix)
```

```python
import functools

import jax
import jax.numpy as jnp
from jax import lax
from jax.experimental import pallas as pl
from jax.experimental.pallas import tpu as pltpu
from jax.sharding import PartitionSpec as P

MESH = pl.DeviceIdType.MESH
NB = 256
SIDE = 4
ZS = 8
ROWS, COLS = 768, 3072
WIDE = COLS + 2 * NB
CHUNK = 768
BIG = SIDE * 16
SHARD = 16
BF = jnp.bfloat16
F32 = jnp.float32


def dot(a, b):
    return jnp.dot(a, b, preferred_element_type=F32)


def turned(row):
    n = row.shape[1]
    i = lax.broadcasted_iota(jnp.int32, (n, n), 0)
    j = lax.broadcasted_iota(jnp.int32, (n, n), 1)
    return jnp.sum(jnp.where(i == j, row, 0), axis=1, keepdims=True)


def kernel(
    a_hbm, piv_ref, li_hbm, ui_hbm, out_hbm,
    a, ap, t, s, ps, po, xr, r1, q, r2, ss, w, lo, d, oh, keep, l0t, x1t, li, ui,
    load_sem, store_sem,
    x_ss, x_rs, r1_ss, r1_rs, r2_ss, r2_rs, s1_ss, s1_rs, s2_ss, s2_rs,
    g1_ss, g1_rs, g2_ss, g2_rs, c_ss, c_rs, z_ss, z_rs, e_ss, e_rs,
):
    row = lax.axis_index("row")
    z = lax.axis_index("col")
    core = lax.rem(row, 2)
    yy = lax.rem(row // 2, SIDE)
    xx = row // (2 * SIDE)
    m = jnp.where(core == 0, xx, yy)
    n = jnp.where(core == 0, yy, xx)

    def at(mm, nn):
        mm, nn = lax.rem(mm + SIDE, SIDE), lax.rem(nn + SIDE, SIDE)
        return (jnp.where(core == 0, mm * SIDE + nn, nn * SIDE + mm) * 2 + core, z)

    sibling = (row + 1 - 2 * core, z)

    def along(k):
        return (row, lax.rem(z + k + ZS, ZS))

    sent = []

    def send(src, dst, ss_, rs_, dev):
        copy = pltpu.make_async_remote_copy(
            src_ref=src, dst_ref=dst, send_sem=ss_, recv_sem=rs_, device_id=dev, device_id_type=MESH
        )
        return copy

    load_a = pltpu.make_async_copy(a_hbm, a, load_sem.at[0])
    load_l = pltpu.make_async_copy(li_hbm, li, load_sem.at[1])
    load_u = pltpu.make_async_copy(ui_hbm, ui, load_sem.at[2])
    load_a.start()
    load_l.start()
    load_u.start()

    barrier = pltpu.get_barrier_semaphore()
    partners = [sibling]
    partners += [at(m + k, n) for k in (1, 2, 3)]
    partners += [at(m, n + k) for k in (1, 2, 3)]
    partners += [along(k) for k in range(1, ZS)]
    for dev in partners:
        pl.semaphore_signal(barrier, inc=1, device_id=dev, device_id_type=MESH)

    p0r, p1r = piv_ref[0:1, :], piv_ref[1:2, :]
    p0c, p1c = turned(p0r), turned(p1r)
    i0 = lax.broadcasted_iota(jnp.int32, (NB, NB), 0)
    i1 = lax.broadcasted_iota(jnp.int32, (NB, NB), 1)
    hit = p1c == p0r
    src1 = jnp.where(
        jnp.max(hit.astype(jnp.int32), axis=1, keepdims=True) > 0,
        jnp.sum(jnp.where(hit, i1, 0), axis=1, keepdims=True),
        p1c,
    )
    src0 = p0c
    inner = p0r == NB + i0
    out_in = jnp.sum(jnp.where(inner, p1c, 0), axis=0, keepdims=True)
    met = jnp.max(hit.astype(jnp.int32), axis=0, keepdims=True) > 0
    met_at = jnp.sum(jnp.where(hit, NB + i0, 0), axis=0, keepdims=True)
    dest0 = jnp.where(p0r < NB, p0r, jnp.where(p0r < 2 * NB, out_in, jnp.where(met, met_at, p0r)))
    back = p0c == NB + i1
    dest1 = jnp.where(
        jnp.max(back.astype(jnp.int32), axis=0, keepdims=True) > 0,
        jnp.sum(jnp.where(back, i0, 0), axis=0, keepdims=True),
        p1r,
    )
    for b in range(ROWS // NB):
        base = b * (NB * 2 * SIDE * SIDE) + row * NB
        rows = pl.ds(b * NB, NB)
        glob_c = base + i0
        glob_r = base + i1
        d0 = dest0 == glob_c
        d1 = dest1 == glob_c
        d[rows, 0:NB] = d0.astype(F32).astype(BF)
        d[rows, NB : 2 * NB] = d1.astype(F32).astype(BF)
        moved = jnp.max(jnp.maximum(d0.astype(F32), d1.astype(F32)), axis=1, keepdims=True)
        keep[rows, :] = jnp.broadcast_to(1.0 - moved, (NB, 128))
        oh[0:NB, b * NB : (b + 1) * NB] = (src0 == glob_r).astype(F32).astype(BF)
        oh[NB : 2 * NB, b * NB : (b + 1) * NB] = (src1 == glob_r).astype(F32).astype(BF)

    load_a.wait()
    pl.semaphore_wait(barrier, len(partners))

    mine = core * NB
    other = NB - mine

    def z_copy(blk, b, to, way, first):
        rows = pl.ds(b * NB, NB)
        cols = pl.ds(blk * NB, NB)
        src = a.at[rows, pl.ds(0, NB)] if first else w.at[rows, cols]
        return send(src, w.at[rows, cols], z_ss.at[blk, b, way], z_rs.at[blk, b], along(to))

    def z_start(blk):
        @pl.when(z == blk)
        def _():
            for b in range(ROWS // NB):
                z_copy(blk, b, 1, 0, True).start()
                z_copy(blk, b, -1, 1, True).start()
            w[:, blk * NB : (blk + 1) * NB] = a[:, 0:NB]

    def z_pass(blk, b):
        rel = lax.rem(z - blk + ZS, ZS)

        @pl.when(rel != 0)
        def _():
            z_copy(blk, b, 1, 0, False).wait_recv()

        @pl.when((rel >= 1) & (rel <= 3))
        def _():
            z_copy(blk, b, 1, 0, False).start()

        @pl.when(rel >= 6)
        def _():
            z_copy(blk, b, -1, 1, False).start()

    def z_end(blk):
        rel = lax.rem(z - blk + ZS, ZS)
        for b in range(ROWS // NB):

            @pl.when(rel <= 3)
            def _():
                z_copy(blk, b, 1, 0, False).wait_send()

            @pl.when((rel == 0) | (rel >= 6))
            def _():
                z_copy(blk, b, -1, 1, False).wait_send()

    root = (m == 0) & (n == 0)

    def s1_copy(k):
        return send(a.at[pl.ds(k * BIG, BIG)], ss, s1_ss.at[k - 1], s1_rs, at(k, 0))

    def s_start():
        @pl.when(root)
        def _():
            for k in (1, 3, 2):
                s1_copy(k).start()
            ss[...] = a[0:BIG, :]

    def shard(mm, nn):
        return pl.ds(pl.multiple_of(mine + mm * BIG + nn * SHARD, SHARD), SHARD)

    def s2_copy(k):
        return send(
            ss.at[pl.ds(k * SHARD, SHARD)], s.at[shard(m, k), pl.ds(0, COLS)],
            s2_ss.at[k - 1], s2_rs, at(m, k),
        )

    def s_second():
        @pl.when((n == 0) & (m != 0))
        def _():
            s1_copy(1).wait_recv()

        @pl.when(n == 0)
        def _():
            for k in (1, 3, 2):
                s2_copy(k).start()
            s[shard(m, 0), 0:COLS] = ss[0:SHARD, :]

    def s_third():
        @pl.when(n != 0)
        def _():
            s2_copy(1).wait_recv()

    def s_end():
        @pl.when(root)
        def _():
            for k in (1, 3, 2):
                s1_copy(k).wait_send()

        @pl.when(n == 0)
        def _():
            for k in (1, 3, 2):
                s2_copy(k).wait_send()

    bufs = (t, s)

    def e_copy(kind, blk, k):
        buf = bufs[kind]
        rows = shard(m, n)
        return send(
            buf.at[rows, pl.ds(0, NB)], buf.at[rows, pl.ds(COLS + blk * NB, NB)],
            e_ss.at[kind, k - 1], e_rs.at[kind, blk], along(k),
        )

    def e_start(kind):
        for blk in range(2):

            @pl.when(z == blk)
            def _():
                for k in (4, 3, 5, 2, 6, 1, 7):
                    e_copy(kind, blk, k).start()
                bufs[kind][shard(m, n), COLS + blk * NB : COLS + (blk + 1) * NB] = bufs[kind][shard(m, n), 0:NB]

    def e_recv(kind):
        for blk in range(2):

            @pl.when(z != blk)
            def _():
                e_copy(kind, blk, 1).wait_recv()

    def e_end(kind):
        @pl.when(z < 2)
        def _():
            for k in range(1, ZS):
                e_copy(kind, 0, k).wait_send()

    def cols_of(c):
        return pl.ds(c * CHUNK, CHUNK)

    def x_copy(c):
        return send(ps.at[:, cols_of(c)], xr.at[:, cols_of(c)], x_ss.at[c], x_rs.at[c], sibling)

    def picks(c):
        def tile(half, into):
            def body(i, carry):
                cc = pl.ds(pl.multiple_of(c * CHUNK + i * NB, NB), NB)
                into[:, cc] = dot(oh[pl.ds(pl.multiple_of(half, NB), NB), :], a[:, cc]).astype(BF)
                return carry

            lax.fori_loop(0, CHUNK // NB, body, 0)

        tile(other, ps)
        x_copy(c).start()
        tile(mine, po)

    def r1_copy(c, k):
        g = lax.rem(m + k, SIDE)
        return send(
            po.at[pl.ds(pl.multiple_of(g * BIG, BIG), BIG), cols_of(c)], r1.at[k - 1, :, cols_of(c)],
            r1_ss.at[c, k - 1], r1_rs.at[c, k - 1], at(m + k, n),
        )

    def reduce_core(c):
        x_copy(c).wait_recv()
        po[:, cols_of(c)] = po[:, cols_of(c)] + xr[:, cols_of(c)]
        for k in (2, 1, 3):
            r1_copy(c, k).start()

    def r2_copy(c, k):
        g = lax.rem(n + k, SIDE)
        return send(
            q.at[pl.ds(pl.multiple_of(g * SHARD, SHARD), SHARD), cols_of(c)], r2.at[k - 1, :, cols_of(c)],
            r2_ss.at[c, k - 1], r2_rs.at[c, k - 1], at(m, n + k),
        )

    def reduce_major(c):
        for k in (1, 3, 2):
            r1_copy(c, k).wait_recv()
        cc = cols_of(c)
        own = po[pl.ds(pl.multiple_of(m * BIG, BIG), BIG), cc]
        q[:, cc] = (own + r1[0, :, cc]) + (r1[1, :, cc] + r1[2, :, cc])
        for k in (2, 1, 3):
            r2_copy(c, k).start()

    def reduce_minor(c):
        for k in (1, 3, 2):
            r2_copy(c, k).wait_recv()
        cc = cols_of(c)
        own = q[pl.ds(pl.multiple_of(n * SHARD, SHARD), SHARD), cc]
        t[shard(m, n), cc] = (own + r2[0, :, cc]) + (r2[1, :, cc] + r2[2, :, cc])

    items = [(1, 0, COLS // 2), (1, COLS // 2, COLS // 2), (1, COLS, 2 * NB), (0, COLS, 2 * NB)]
    first_t = len(items)
    items += [(0, c * CHUNK, CHUNK) for c in range(COLS // CHUNK)]

    def g1_copy(i, k):
        kind, c0, width = items[i]
        part = bufs[kind].at[shard(m, n), pl.ds(c0, width)]
        return send(part, part, g1_ss.at[i, k - 1], g1_rs.at[i, k - 1], at(m, n + k))

    def gather_minor(i):
        for k in (2, 1, 3):
            g1_copy(i, k).start()

    def block(mm):
        return pl.ds(pl.multiple_of(mine + lax.rem(mm + SIDE, SIDE) * BIG, BIG), BIG)

    ways = ((0, 0, 1), (0, 1, -1), (0, 1, 1), (0, 0, -1), (-1, 0, 1), (1, 1, -1))

    def g2_copy(i, j):
        kind, c0, width = items[i]
        who, half, way = ways[j]
        part = bufs[kind].at[block(m + who), pl.ds(c0 + half * (width // 2), width // 2)]
        return send(part, part, g2_ss.at[i, j], g2_rs.at[i, j], at(m + way, n))

    def gather_major(i):
        for k in (1, 3, 2):
            g1_copy(i, k).wait_recv()
        for j in range(4):
            g2_copy(i, j).start()

    def gather_pass(i):
        g2_copy(i, 0).wait_recv()
        g2_copy(i, 4).start()
        g2_copy(i, 1).wait_recv()
        g2_copy(i, 5).start()

    def c_copy(i):
        kind, c0, width = items[i]
        part = bufs[kind].at[pl.ds(pl.multiple_of(mine, NB), NB), pl.ds(c0, width)]
        return send(part, part, c_ss.at[i], c_rs.at[i], sibling)

    def gather_core(i):
        for j in (2, 3, 4, 5):
            g2_copy(i, j).wait_recv()
        c_copy(i).start()

    def gathered(i):
        c_copy(i).wait_recv()

    def displaced(c0, width):
        def body(i, carry):
            cc = pl.ds(pl.multiple_of(c0 + i * NB, NB), NB)
            for b in range(ROWS // NB):
                rows = pl.ds(b * NB, NB)
                stay = jnp.concatenate([keep[rows, :], keep[rows, :]], axis=1) > 0.5
                arriving = dot(d[rows, :], s[:, cc])
                ap[rows, cc] = jnp.where(stay, a[rows, cc].astype(F32), arriving).astype(BF)
            return carry

        lax.fori_loop(0, width // NB, body, 0)

    def lowers():
        l0t[...] = dot(t[NB : 2 * NB, COLS : COLS + NB], ui[0]).astype(BF)
        u0w = dot(li[0], t[0:NB, COLS + NB : WIDE]).astype(BF)
        x1t[...] = (t[NB : 2 * NB, COLS + NB : WIDE].astype(F32) - dot(l0t[...], u0w)).astype(BF)

        def body(b, carry):
            rows = pl.ds(pl.multiple_of(b * NB, NB), NB)
            stay = jnp.concatenate([keep[rows, :], keep[rows, :]], axis=1) > 0.5
            w0 = jnp.where(stay, w[rows, 0:NB].astype(F32), dot(d[rows, :], s[:, COLS : COLS + NB])).astype(BF)
            w1 = jnp.where(stay, w[rows, NB : 2 * NB].astype(F32), dot(d[rows, :], s[:, COLS + NB : WIDE]))
            low0 = dot(w0, ui[0]).astype(BF)
            x1 = (w1 - dot(low0, u0w)).astype(BF)
            lo[rows, 0:NB] = low0
            lo[rows, NB : 2 * NB] = dot(x1, ui[1]).astype(BF)
            return carry

        lax.fori_loop(0, ROWS // NB, body, 0)

    def update(c):
        def body(i, carry):
            cc = pl.ds(pl.multiple_of(c * CHUNK + i * NB, NB), NB)
            u0 = dot(li[0], t[0:NB, cc]).astype(BF)
            x1 = (t[NB : 2 * NB, cc].astype(F32) - dot(l0t[...], u0)).astype(BF)
            u1 = dot(li[1], x1).astype(BF)
            uu = jnp.concatenate([u0, u1], axis=0)
            ap[:, cc] = (ap[:, cc].astype(F32) - dot(lo[...], uu)).astype(BF)

            @pl.when(row == 0)
            def _():
                ap[0:NB, cc] = u0

            @pl.when(row == 1)
            def _():
                ap[0:NB, cc] = u1

            return carry

        lax.fori_loop(0, CHUNK // NB, body, 0)
        if c == 0:

            @pl.when((z == 0) & (row > 0))
            def _():
                ap[0:NB, 0:NB] = lo[0:NB, 0:NB]

            @pl.when((z == 1) & (row > 1))
            def _():
                ap[0:NB, 0:NB] = lo[0:NB, NB : 2 * NB]

            @pl.when(z == 0)
            def _():
                ap[NB:ROWS, 0:NB] = lo[NB:ROWS, 0:NB]

            @pl.when(z == 1)
            def _():
                ap[NB:ROWS, 0:NB] = lo[NB:ROWS, NB : 2 * NB]

            @pl.when((z == 0) & (row == 0))
            def _():
                ap[0:NB, 0:NB] = t[0:NB, 0:NB]

            @pl.when((z == 0) & (row == 1))
            def _():
                ap[0:NB, 0:NB] = l0t[...]

            @pl.when((z == 1) & (row == 1))
            def _():
                ap[0:NB, 0:NB] = x1t[...]

    def store(c):
        return pltpu.make_async_copy(ap.at[:, cols_of(c)], out_hbm.at[:, cols_of(c)], store_sem.at[c])

    chunks = COLS // CHUNK
    s_start()
    z_start(0)
    z_start(1)
    picks(0)
    for c in range(1, chunks):
        picks(c)
        reduce_core(c - 1)
    reduce_core(chunks - 1)
    for b in range(ROWS // NB):
        z_pass(1, b)
        z_pass(0, b)
    reduce_major(0)
    s_second()
    reduce_major(1)
    reduce_minor(0)
    e_start(0)
    s_third()
    e_start(1)
    gather_minor(0)
    gather_minor(1)
    reduce_major(2)
    reduce_minor(1)
    e_recv(1)
    gather_minor(2)
    e_recv(0)
    gather_minor(3)
    gather_minor(4)
    gather_major(0)
    reduce_major(3)
    gather_minor(5)
    gather_major(1)
    reduce_minor(2)
    gather_minor(6)
    gather_pass(0)
    reduce_minor(3)
    gather_minor(7)
    gather_major(2)
    gather_major(3)
    gather_pass(1)
    gather_major(4)
    gather_pass(2)
    gather_pass(3)
    gather_core(0)
    gather_major(5)
    gather_core(1)
    gather_pass(4)
    gather_core(2)
    gather_core(3)
    gather_major(6)
    gathered(0)
    displaced(0, COLS // 2)
    gather_pass(5)
    gather_core(4)
    gather_major(7)
    gathered(1)
    displaced(COLS // 2, COLS // 2)
    gather_pass(6)
    gather_core(5)
    gathered(2)
    gathered(3)
    load_l.wait()
    load_u.wait()
    lowers()
    gather_pass(7)
    gather_core(6)
    gathered(4)
    update(0)
    store(0).start()
    gathered(5)
    update(1)
    store(1).start()
    gather_core(7)
    gathered(6)
    update(2)
    store(2).start()
    gathered(7)
    update(3)
    store(3).start()

    s_end()
    z_end(0)
    z_end(1)
    e_end(0)
    e_end(1)
    for c in range(chunks):
        x_copy(c).wait_send()
        for k in (1, 2, 3):
            r1_copy(c, k).wait_send()
            r2_copy(c, k).wait_send()
    for i in range(len(items)):
        for k in (1, 2, 3):
            g1_copy(i, k).wait_send()
        for j in range(6):
            g2_copy(i, j).wait_send()
        c_copy(i).wait_send()
    for c in range(chunks):
        store(c).wait()


def per_device(a_stored, pivots, l_inverse, u_inverse):
    chunks = COLS // CHUNK
    n_items = 4 + chunks
    dma = pltpu.SemaphoreType.DMA
    anyspace = pl.BlockSpec(memory_space=pl.ANY)
    scratch = [
        pltpu.VMEM((ROWS, COLS), BF),
        pltpu.VMEM((ROWS, COLS), BF),
        pltpu.VMEM((2 * NB, WIDE), BF),
        pltpu.VMEM((2 * NB, WIDE), BF),
        pltpu.VMEM((NB, COLS), BF),
        pltpu.VMEM((NB, COLS), BF),
        pltpu.VMEM((NB, COLS), BF),
        pltpu.VMEM((3, BIG, COLS), BF),
        pltpu.VMEM((BIG, COLS), BF),
        pltpu.VMEM((3, SHARD, COLS), BF),
        pltpu.VMEM((BIG, COLS), BF),
        pltpu.VMEM((ROWS, 2 * NB), BF),
        pltpu.VMEM((ROWS, 2 * NB), BF),
        pltpu.VMEM((ROWS, 2 * NB), BF),
        pltpu.VMEM((2 * NB, ROWS), BF),
        pltpu.VMEM((ROWS, 128), F32),
        pltpu.VMEM((NB, NB), BF),
        pltpu.VMEM((NB, NB), BF),
        pltpu.VMEM((2, NB, NB), BF),
        pltpu.VMEM((2, NB, NB), BF),
        dma((3,)), dma((chunks,)),
        dma((chunks,)), dma((chunks,)),
        dma((chunks, 3)), dma((chunks, 3)),
        dma((chunks, 3)), dma((chunks, 3)),
        dma((3,)), dma,
        dma((3,)), dma,
        dma((n_items, 3)), dma((n_items, 3)),
        dma((n_items, 6)), dma((n_items, 6)),
        dma((n_items,)), dma((n_items,)),
        dma((2, 3, 2)), dma((2, 3)),
        dma((2, ZS - 1)), dma((2, 2)),
    ]
    return pl.pallas_call(
        kernel,
        out_shape=jax.ShapeDtypeStruct((ROWS, COLS), BF),
        in_specs=[anyspace, pl.BlockSpec(memory_space=pltpu.VMEM), anyspace, anyspace],
        out_specs=anyspace,
        scratch_shapes=scratch,
        compiler_params=pltpu.CompilerParams(
            collective_id=0, has_side_effects=True, vmem_limit_bytes=48 * 2**20
        ),
        name="panels",
    )(a_stored, pivots, l_inverse, u_inverse)


def solution(mesh):
    in_specs = (P("row", "col"), P(), P(), P())
    out_specs = P("row", "col")
    return jax.shard_map(
        per_device, mesh=mesh, in_specs=in_specs, out_specs=out_specs, check_vma=False
    )
```

```python
import functools

import jax
import jax.numpy as jnp
from jax import lax
from jax.experimental import pallas as pl
from jax.experimental.pallas import tpu as pltpu
from jax.sharding import PartitionSpec as P

MESH = pl.DeviceIdType.MESH
NB = 256
SIDE = 4
ZS = 8
ROWS, COLS = 768, 3072
WIDTHS = (768, 768, 768, 768)
STARTS = tuple(sum(WIDTHS[:c]) for c in range(len(WIDTHS)))
CHUNKS = range(len(WIDTHS))
S_WIDTHS = (256, 768, 768, 768, 512)
S_STARTS = tuple(sum(S_WIDTHS[:c]) for c in range(len(S_WIDTHS)))
S_CHUNKS = range(len(S_WIDTHS))
TREE = (
    (1, 0, 0, 1), (1, 1, 1, 2), (1, 3, 3, 2), (2, 0, 0, 2), (0, 1, 2, 3), (0, 3, 2, 3), (1, 2, 3, 3), (2, 1, 1, 3),
    (2, 3, 0, 3), (3, 0, 0, 3), (0, 2, 2, 4), (2, 2, 1, 4), (3, 1, 0, 4), (3, 3, 0, 4), (3, 2, 0, 5),
)
DEPTH = 5
STEP_X, STEP_Y = (1, 0, -1, 0), (0, 1, 0, -1)
HALF = NB // 2
PLAN = (
    "v1", "picks0", "picks1", "v2", "core0", "z1", "core1", "picks2", "v3", "picks3", "places", "major0", "core2",
    "z2", "major1", "minor0", "n.T0", "et", "v4", "core3", "z3", "major2", "ert", "n.TE", "m.T0", "v5", "minor1",
    "es", "n.T1", "m.TE", "p.T0", "major3", "z4", "c.S0", "ers", "n.SE", "minor2", "n.T2", "p.TE", "m.T1", "c.T0",
    "v6", "minor3", "m.SE", "c.TE", "p.T1", "n.T3", "z5", "g.TE", "g.T0", "lowtop", "p.SE", "m.T2", "c.S1", "c.T1",
    "v7", "c.S2", "m.T3", "uppers0", "c.SE", "p.T2", "g.T1", "uppers1", "z6", "g.S0", "p.T3", "g.S1", "g.S2",
    "g.SE", "lowers", "c.T2", "v8", "update0", "update1", "g.T2", "c.T3", "uppers2", "c.S3", "v9", "c.S4",
    "update2", "g.T3", "uppers3", "g.S3", "update3", "g.S4", "update4",
)
BIG = SIDE * 16
SHARD = 16
BF = jnp.bfloat16
F32 = jnp.float32


def dot(a, b):
    return jnp.dot(a, b, preferred_element_type=F32)


def turned(row):
    n = row.shape[1]
    i = lax.broadcasted_iota(jnp.int32, (n, n), 0)
    j = lax.broadcasted_iota(jnp.int32, (n, n), 1)
    return jnp.sum(jnp.where(i == j, row, 0), axis=1, keepdims=True)


def kernel(
    a_hbm, piv_hbm, li_hbm, ui_hbm, ap,
    a, t, su, ps, po, xr, r1, q, r2, w, dl, oh, keep, l0t, u0w, li, ui, piv_ref,
    load_sem, part_sem,
    x_ss, x_rs, r1_ss, r1_rs, r2_ss, r2_rs, v_ss, v_rs,
    g1_ss, g1_rs, g2_ss, g2_rs, c_ss, c_rs, z_ss, z_rs, e_ss, e_rs,
):
    row = lax.axis_index("row")
    z = lax.axis_index("col")
    core = lax.rem(row, 2)
    yy = lax.rem(row // 2, SIDE)
    xx = row // (2 * SIDE)
    m = jnp.where(core == 0, xx, yy)
    n = jnp.where(core == 0, yy, xx)

    def at(mm, nn):
        mm, nn = lax.rem(mm + SIDE, SIDE), lax.rem(nn + SIDE, SIDE)
        return (jnp.where(core == 0, mm * SIDE + nn, nn * SIDE + mm) * 2 + core, z)

    sibling = (row + 1 - 2 * core, z)

    def along(k):
        return (row, lax.rem(z + k + ZS, ZS))

    s = su.at[pl.ds(0, 2 * NB)]

    def send(src, dst, ss_, rs_, dev):
        return pltpu.make_async_remote_copy(
            src_ref=src, dst_ref=dst, send_sem=ss_, recv_sem=rs_, device_id=dev, device_id_type=MESH
        )

    def load_a(c):
        cc = pl.ds(STARTS[c], WIDTHS[c])
        return pltpu.make_async_copy(a_hbm.at[:, cc], a.at[:, cc], part_sem.at[c])

    load_l = pltpu.make_async_copy(li_hbm, li, load_sem.at[1])
    load_u = pltpu.make_async_copy(ui_hbm, ui, load_sem.at[2])
    load_p = pltpu.make_async_copy(piv_hbm, piv_ref, load_sem.at[3])
    load_p.start()
    for c in CHUNKS:
        load_a(c).start()
    load_l.start()
    load_u.start()

    barrier = pltpu.get_barrier_semaphore()
    partners = [sibling]
    partners += [at(m + k, n) for k in (1, 2, 3)]
    partners += [at(m, n + k) for k in (1, 2, 3)]
    partners += [along(k) for k in range(1, ZS)]
    for dev in partners:
        pl.semaphore_signal(barrier, inc=1, device_id=dev, device_id_type=MESH)

    pl.semaphore_wait(barrier, len(partners))

    mine = core * NB

    def z_copy(blk, b, to, way, first):
        rows = pl.ds(b * NB, NB)
        cols = pl.ds(blk * NB, NB)
        src = a_hbm.at[rows, pl.ds(0, NB)] if first else w.at[rows, cols]
        return send(src, w.at[rows, cols], z_ss.at[blk, b, way], z_rs.at[blk, b], along(to))

    def own_panel(blk):
        return pltpu.make_async_copy(a_hbm.at[:, pl.ds(0, NB)], w.at[:, pl.ds(blk * NB, NB)], load_sem.at[4])

    def z_start(blk):
        @pl.when(z == blk)
        def _():
            for b in range(ROWS // NB):
                z_copy(blk, b, 1, 0, True).start()
                z_copy(blk, b, -1, 1, True).start()
            own_panel(blk).start()

    def z_wave(wave):
        for blk in (1, 0):
            rel = lax.rem(z - blk + ZS, ZS)
            for b in range(ROWS // NB):
                hops = wave - b
                if 1 <= hops <= 4:

                    @pl.when(rel == hops)
                    def _():
                        z_copy(blk, b, 1, 0, False).wait_recv()
                        if hops < 4:
                            z_copy(blk, b, 1, 0, False).start()

                if 1 <= hops <= 3:

                    @pl.when(rel == ZS - hops)
                    def _():
                        z_copy(blk, b, 1, 0, False).wait_recv()
                        if hops < 3:
                            z_copy(blk, b, -1, 1, False).start()

    def z_end(blk):
        rel = lax.rem(z - blk + ZS, ZS)

        for b in range(ROWS // NB):

            @pl.when(rel <= 3)
            def _():
                z_copy(blk, b, 1, 0, False).wait_send()

            @pl.when((rel == 0) | (rel >= 6))
            def _():
                z_copy(blk, b, -1, 1, False).wait_send()

    root = (m == 0) & (n == 0)

    def shard(mm, nn):
        return pl.ds(pl.multiple_of(mine + mm * BIG + nn * SHARD, SHARD), SHARD)

    own_rows = pltpu.make_async_copy(
        a_hbm.at[pl.ds(0, NB)], su.at[pl.ds(pl.multiple_of(mine, NB), NB), pl.ds(0, COLS)], load_sem.at[5]
    )
    flip = 1 - 2 * core

    depths, passes = [], []
    for sign in (1, -1):
        px = lax.rem(sign * m + SIDE, SIDE)
        py = lax.rem(sign * flip * n + SIDE, SIDE)
        depth = 0
        go = [False] * 4
        for x, y, way, h in TREE:
            depth = depth + jnp.where((px == x) & (py == y), h, 0)
            go[way] = go[way] | ((px == (x - STEP_X[way]) % SIDE) & (py == (y - STEP_Y[way]) % SIDE))
        depths.append(depth)
        passes.append(go)

    def v_copy(tree, b, way, first=False):
        sign = 1 - 2 * tree
        cols = pl.ds(S_STARTS[b], S_WIDTHS[b])
        dst = su.at[pl.ds(pl.multiple_of(mine + tree * HALF, HALF), HALF), cols]
        src = a_hbm.at[pl.ds(tree * HALF, HALF), cols] if first else dst
        to = at(m + sign * STEP_X[way], n + sign * flip * STEP_Y[way])
        return send(src, dst, v_ss.at[tree, b, way], v_rs.at[tree, b], to)

    def s_start():
        @pl.when(root)
        def _():
            own_rows.start()
            for b in S_CHUNKS:
                for tree in range(2):
                    v_copy(tree, b, 0, True).start()

    def s_wave(wave):
        for b in S_CHUNKS:
            hops = wave - b
            if not 1 <= hops <= DEPTH:
                continue
            for tree in range(2):

                @pl.when(depths[tree] == hops)
                def _():
                    v_copy(tree, b, 0).wait_recv()
                    for way in range(4):
                        if any(h == hops + 1 and e == way for _, _, e, h in TREE):

                            @pl.when(passes[tree][way])
                            def _():
                                v_copy(tree, b, way).start()

        if wave == 1:

            @pl.when(root)
            def _():
                own_rows.wait()

    def s_end():
        for tree in range(2):
            for b in S_CHUNKS:
                for way in range(4):

                    @pl.when(passes[tree][way])
                    def _():
                        v_copy(tree, b, way).wait_send()

    bufs = (t, s)

    def e_copy(kind, blk, k):
        rows = shard(m, n)
        buf = bufs[kind]
        to = COLS + blk * NB if kind else COLS
        return send(
            buf.at[rows, pl.ds(0, NB)], buf.at[rows, pl.ds(to, NB)], e_ss.at[kind, k - 1], e_rs.at[kind, blk], along(k)
        )

    def e_sources(kind):
        return ((0, z == 0), (1, z == 1)) if kind else ((0, z == 1 - core),)

    def e_start(kind):
        for blk, here in e_sources(kind):

            @pl.when(here)
            def _():
                for k in (4, 3, 5, 2, 6, 1, 7):
                    e_copy(kind, blk, k).start()
                to = COLS + blk * NB if kind else COLS
                bufs[kind][shard(m, n), to : to + NB] = bufs[kind][shard(m, n), 0:NB]

    def e_recv(kind):
        for blk, here in e_sources(kind):

            @pl.when(jnp.logical_not(here))
            def _():
                e_copy(kind, blk, 1).wait_recv()

    def e_end(kind):
        for blk, here in e_sources(kind):

            @pl.when(here)
            def _():
                for k in range(1, ZS):
                    e_copy(kind, blk, k).wait_send()

    def cols_of(c):
        return pl.ds(STARTS[c], WIDTHS[c])

    def x_copy(c):
        return send(ps.at[:, cols_of(c)], xr.at[:, cols_of(c)], x_ss.at[c], x_rs.at[c], sibling)

    def picks(c):
        load_a(c).wait()

        def body(i, carry):
            cc = pl.ds(pl.multiple_of(STARTS[c] + i * NB, NB), NB)
            both = dot(oh[...], a[:, cc]).astype(BF)
            ps[:, cc] = both[0:NB]
            po[:, cc] = both[NB : 2 * NB]
            return carry

        lax.fori_loop(0, WIDTHS[c] // NB, body, 0)
        x_copy(c).start()

    def r1_copy(c, k):
        g = lax.rem(m + k, SIDE)
        return send(
            po.at[pl.ds(pl.multiple_of(g * BIG, BIG), BIG), cols_of(c)], r1.at[k - 1, :, cols_of(c)],
            r1_ss.at[c, k - 1], r1_rs.at[c, k - 1], at(m + k, n),
        )

    def reduce_core(c):
        x_copy(c).wait_recv()
        po[:, cols_of(c)] = po[:, cols_of(c)] + xr[:, cols_of(c)]
        for k in (2, 1, 3):
            r1_copy(c, k).start()

    def r2_copy(c, k):
        g = lax.rem(n + k, SIDE)
        return send(
            q.at[pl.ds(pl.multiple_of(g * SHARD, SHARD), SHARD), cols_of(c)], r2.at[k - 1, :, cols_of(c)],
            r2_ss.at[c, k - 1], r2_rs.at[c, k - 1], at(m, n + k),
        )

    def reduce_major(c):
        for k in (1, 3, 2):
            r1_copy(c, k).wait_recv()
        cc = cols_of(c)
        own = po[pl.ds(pl.multiple_of(m * BIG, BIG), BIG), cc]
        q[:, cc] = (own + r1[0, :, cc]) + (r1[1, :, cc] + r1[2, :, cc])
        for k in (2, 1, 3):
            r2_copy(c, k).start()

    def reduce_minor(c):
        for k in (1, 3, 2):
            r2_copy(c, k).wait_recv()
        cc = cols_of(c)
        own = q[pl.ds(pl.multiple_of(n * SHARD, SHARD), SHARD), cc]
        t[shard(m, n), cc] = (own + r2[0, :, cc]) + (r2[1, :, cc] + r2[2, :, cc])

    items = [(1, S_STARTS[c], S_WIDTHS[c]) for c in S_CHUNKS] + [(1, COLS, 2 * NB), (0, COLS, NB)]
    items += [(0, STARTS[c], WIDTHS[c]) for c in CHUNKS]

    def g1_copy(i, k):
        kind, c0, width = items[i]
        part = bufs[kind].at[shard(m, n), pl.ds(c0, width)]
        return send(part, part, g1_ss.at[i, k - 1], g1_rs.at[i, k - 1], at(m, n + k))

    def gather_minor(i):
        for k in (2, 1, 3):
            g1_copy(i, k).start()

    def block(mm):
        return pl.ds(pl.multiple_of(mine + lax.rem(mm + SIDE, SIDE) * BIG, BIG), BIG)

    ways = ((0, 0, 1), (0, 1, -1), (0, 1, 1), (0, 0, -1), (-1, 0, 1), (1, 1, -1))

    def g2_copy(i, j):
        kind, c0, width = items[i]
        who, half, way = ways[j]
        part = bufs[kind].at[block(m + who), pl.ds(c0 + half * (width // 2), width // 2)]
        return send(part, part, g2_ss.at[i, j], g2_rs.at[i, j], at(m + way, n))

    def gather_major(i):
        for k in (1, 3, 2):
            g1_copy(i, k).wait_recv()
        for j in range(4):
            g2_copy(i, j).start()

    def gather_pass(i):
        g2_copy(i, 0).wait_recv()
        g2_copy(i, 4).start()
        g2_copy(i, 1).wait_recv()
        g2_copy(i, 5).start()

    def c_copy(i):
        kind, c0, width = items[i]
        part = bufs[kind].at[pl.ds(pl.multiple_of(mine, NB), NB), pl.ds(c0, width)]
        return send(part, part, c_ss.at[i], c_rs.at[i], sibling)

    def gather_core(i):
        if i >= len(S_WIDTHS):
            for j in (2, 3, 4, 5):
                g2_copy(i, j).wait_recv()
        c_copy(i).start()

    def gathered(i):
        c_copy(i).wait_recv()

    def lowtop():
        load_l.wait()
        load_u.wait()
        l0t[...] = dot(t[NB : 2 * NB, COLS : COLS + NB], ui[0]).astype(BF)
        u0w[...] = dot(li[0], t[0:NB, COLS : COLS + NB]).astype(BF)

    def lowers():
        for blk in range(2):

            @pl.when(z == blk)
            def _():
                own_panel(blk).wait()

        def body(b, carry):
            rows = pl.ds(pl.multiple_of(b * NB, NB), NB)
            stay = jnp.concatenate([keep[rows, :], keep[rows, :]], axis=1) > 0.5
            take = dl[rows, 0 : 2 * NB]
            w0 = jnp.where(stay, w[rows, 0:NB].astype(F32), dot(take, s[:, COLS : COLS + NB])).astype(BF)
            w1 = jnp.where(stay, w[rows, NB : 2 * NB].astype(F32), dot(take, s[:, COLS + NB : COLS + 2 * NB]))
            low0 = dot(w0, ui[0]).astype(BF)
            x1 = (w1 - dot(low0, u0w[...])).astype(BF)
            dl[rows, 2 * NB : 3 * NB] = -low0
            dl[rows, 3 * NB : 4 * NB] = -dot(x1, ui[1]).astype(BF)
            return carry

        lax.fori_loop(0, ROWS // NB, body, 0)

    def uppers(c):
        cc = cols_of(c)
        u0 = dot(li[0], t[0:NB, cc]).astype(BF)
        su[2 * NB : 3 * NB, cc] = u0
        x1 = (t[NB : 2 * NB, cc].astype(F32) - dot(l0t[...], u0)).astype(BF)
        su[3 * NB : 4 * NB, cc] = dot(li[1], x1).astype(BF)

    def update(c):
        def body(i, carry):
            cc = pl.ds(pl.multiple_of(S_STARTS[c] + i * NB, NB), NB)
            stay = jnp.concatenate([keep[...], keep[...]], axis=1) > 0.5
            base = jnp.where(stay, a[:, cc].astype(F32), 0.0)
            ap[:, cc] = (base + dot(dl[...], su[:, cc])).astype(BF)
            return carry

        lax.fori_loop(0, S_WIDTHS[c] // NB, body, 0)
        cc = pl.ds(S_STARTS[c], S_WIDTHS[c])

        @pl.when(row == 0)
        def _():
            ap[0:NB, cc] = su[2 * NB : 3 * NB, cc]

        @pl.when(row == 1)
        def _():
            ap[0:NB, cc] = su[3 * NB : 4 * NB, cc]

        if c == 0:
            panel_out()

    def panel_out():
        @pl.when((z == 0) & (row > 0))
        def _():
            ap[0:NB, 0:NB] = -dl[0:NB, 2 * NB : 3 * NB]

        @pl.when((z == 1) & (row > 1))
        def _():
            ap[0:NB, 0:NB] = -dl[0:NB, 3 * NB : 4 * NB]

        @pl.when(z == 0)
        def _():
            ap[NB:ROWS, 0:NB] = -dl[NB:ROWS, 2 * NB : 3 * NB]

        @pl.when(z == 1)
        def _():
            ap[NB:ROWS, 0:NB] = -dl[NB:ROWS, 3 * NB : 4 * NB]

        @pl.when((z == 0) & (row == 0))
        def _():
            ap[0:NB, 0:NB] = t[0:NB, 0:NB]

        @pl.when((z == 0) & (row == 1))
        def _():
            ap[0:NB, 0:NB] = l0t[...]

        @pl.when((z == 1) & (row == 1))
        def _():
            ap[0:NB, 0:NB] = (t[NB : 2 * NB, 0:NB].astype(F32) - dot(l0t[...], u0w[...])).astype(BF)

    s_start()
    z_start(0)
    z_start(1)

    load_p.wait()
    p0r, p1r = piv_ref[0:1, :], piv_ref[1:2, :]
    p0c, p1c = turned(p0r), turned(p1r)
    i0 = lax.broadcasted_iota(jnp.int32, (NB, NB), 0)
    i1 = lax.broadcasted_iota(jnp.int32, (NB, NB), 1)
    hit = p1c == p0r
    src1 = jnp.where(
        jnp.max(hit.astype(jnp.int32), axis=1, keepdims=True) > 0,
        jnp.sum(jnp.where(hit, i1, 0), axis=1, keepdims=True),
        p1c,
    )
    src_other = jnp.where(core == 0, src1, p0c)
    src_mine = jnp.where(core == 0, p0c, src1)
    for b in range(ROWS // NB):
        glob_r = b * (NB * 2 * SIDE * SIDE) + row * NB + i1
        oh[0:NB, b * NB : (b + 1) * NB] = (src_other == glob_r).astype(F32).astype(BF)
        oh[NB : 2 * NB, b * NB : (b + 1) * NB] = (src_mine == glob_r).astype(F32).astype(BF)

    def places():
        inner = p0r == NB + i0
        out_in = jnp.sum(jnp.where(inner, p1c, 0), axis=0, keepdims=True)
        met = jnp.max(hit.astype(jnp.int32), axis=0, keepdims=True) > 0
        met_at = jnp.sum(jnp.where(hit, NB + i0, 0), axis=0, keepdims=True)
        dest0 = jnp.where(p0r < NB, p0r, jnp.where(p0r < 2 * NB, out_in, jnp.where(met, met_at, p0r)))
        back = p0c == NB + i1
        dest1 = jnp.where(
            jnp.max(back.astype(jnp.int32), axis=0, keepdims=True) > 0,
            jnp.sum(jnp.where(back, i0, 0), axis=0, keepdims=True),
            p1r,
        )
        for b in range(ROWS // NB):
            rows = pl.ds(b * NB, NB)
            glob_c = b * (NB * 2 * SIDE * SIDE) + row * NB + i0
            d0 = dest0 == glob_c
            d1 = dest1 == glob_c
            dl[rows, 0:NB] = d0.astype(F32).astype(BF)
            dl[rows, NB : 2 * NB] = d1.astype(F32).astype(BF)
            moved = jnp.max(jnp.maximum(d0.astype(F32), d1.astype(F32)), axis=1, keepdims=True)
            keep[rows, :] = jnp.broadcast_to(1.0 - moved, (NB, 128))

    names = ["S%d" % c for c in S_CHUNKS] + ["SE", "TE"] + ["T%d" % c for c in CHUNKS]
    gathers = {"n": gather_minor, "m": gather_major, "p": gather_pass, "c": gather_core, "g": gathered}
    stages = {
        "picks": picks, "core": reduce_core, "major": reduce_major, "minor": reduce_minor,
        "uppers": uppers, "update": update, "z": z_wave, "v": s_wave,
    }
    single = {
        "et": (e_start, 0), "es": (e_start, 1), "ert": (e_recv, 0), "ers": (e_recv, 1),
        "lowers": (lowers,), "lowtop": (lowtop,), "places": (places,),
    }
    steps = []
    for word in PLAN:
        if "." in word:
            steps.append((gathers[word[0]], names.index(word[2:])))
        elif word in single:
            steps.append(single[word])
        else:
            steps.append((stages[word[:-1]], int(word[-1])))
    for step, *which in steps:
        step(*which)

    s_end()
    z_end(0)
    z_end(1)
    e_end(0)
    e_end(1)
    for c in CHUNKS:
        x_copy(c).wait_send()
        for k in (1, 2, 3):
            r1_copy(c, k).wait_send()
            r2_copy(c, k).wait_send()
    for i in range(len(items)):
        c_copy(i).wait_send()
    for i in range(len(S_WIDTHS), len(items)):
        for k in (1, 2, 3):
            g1_copy(i, k).wait_send()
        for j in range(6):
            g2_copy(i, j).wait_send()


def per_device(a_stored, pivots, l_inverse, u_inverse):
    chunks = len(WIDTHS)
    n_items = 2 + chunks + len(S_WIDTHS)
    dma = pltpu.SemaphoreType.DMA
    hbm = pl.BlockSpec(memory_space=pltpu.HBM)
    scratch = [
        pltpu.VMEM((ROWS, COLS), BF),
        pltpu.VMEM((2 * NB, COLS + NB), BF),
        pltpu.VMEM((4 * NB, COLS + 2 * NB), BF),
        pltpu.VMEM((NB, COLS), BF),
        pltpu.VMEM((NB, COLS), BF),
        pltpu.VMEM((NB, COLS), BF),
        pltpu.VMEM((3, BIG, COLS), BF),
        pltpu.VMEM((BIG, COLS), BF),
        pltpu.VMEM((3, SHARD, COLS), BF),
        pltpu.VMEM((ROWS, 2 * NB), BF),
        pltpu.VMEM((ROWS, 4 * NB), BF),
        pltpu.VMEM((2 * NB, ROWS), BF),
        pltpu.VMEM((ROWS, 128), F32),
        pltpu.VMEM((NB, NB), BF),
        pltpu.VMEM((NB, NB), BF),
        pltpu.VMEM((2, NB, NB), BF),
        pltpu.VMEM((2, NB, NB), BF),
        pltpu.VMEM((2, NB), jnp.int32),
        dma((6,)), dma((chunks,)),
        dma((chunks,)), dma((chunks,)),
        dma((chunks, 3)), dma((chunks, 3)),
        dma((chunks, 3)), dma((chunks, 3)),
        dma((2, len(S_WIDTHS), 4)), dma((2, len(S_WIDTHS))),
        dma((n_items, 3)), dma((n_items, 3)),
        dma((n_items, 6)), dma((n_items, 6)),
        dma((n_items,)), dma((n_items,)),
        dma((2, 3, 2)), dma((2, 3)),
        dma((2, ZS - 1)), dma((2, 2)),
    ]
    return pl.pallas_call(
        kernel,
        out_shape=jax.ShapeDtypeStruct((ROWS, COLS), BF),
        in_specs=[hbm] * 4,
        out_specs=pl.BlockSpec(memory_space=pltpu.VMEM),
        scratch_shapes=scratch,
        compiler_params=pltpu.CompilerParams(
            collective_id=0, has_side_effects=True, vmem_limit_bytes=48 * 2**20
        ),
        name="panels",
    )(a_stored, pivots, l_inverse, u_inverse)


def solution(mesh):
    in_specs = (P("row", "col"), P(), P(), P())
    out_specs = P("row", "col")
    return jax.shard_map(
        per_device, mesh=mesh, in_specs=in_specs, out_specs=out_specs, check_vma=False
    )
```

```python
import functools

import jax
import jax.numpy as jnp
from jax import lax
from jax.experimental import pallas as pl
from jax.experimental.pallas import tpu as pltpu
from jax.sharding import PartitionSpec as P

MESH = pl.DeviceIdType.MESH
NB = 256
SIDE = 4
ZS = 8
ROWS, COLS = 768, 3072
WIDTHS = (768, 768, 768, 768)
STARTS = tuple(sum(WIDTHS[:c]) for c in range(len(WIDTHS)))
CHUNKS = range(len(WIDTHS))
S_WIDTHS = (768, 768, 768, 768)
S_STARTS = tuple(sum(S_WIDTHS[:c]) for c in range(len(S_WIDTHS)))
S_CHUNKS = range(len(S_WIDTHS))
TREE = (
    (1, 0, 0, 1), (1, 1, 1, 2), (1, 3, 3, 2), (2, 0, 0, 2), (0, 1, 2, 3), (0, 3, 2, 3), (1, 2, 3, 3), (2, 1, 1, 3),
    (2, 3, 0, 3), (3, 0, 0, 3), (0, 2, 2, 4), (2, 2, 1, 4), (3, 1, 0, 4), (3, 3, 0, 4), (3, 2, 0, 5),
)
DEPTH = 5
STEP_X, STEP_Y = (1, 0, -1, 0), (0, 1, 0, -1)
HALF = NB // 2
PLAN = (
    "picks0", "v1", "picks1", "z1", "es", "core0", "picks2", "v2", "core1", "picks3", "places", "z2", "ers", "n.SE",
    "major0", "core2", "v3", "major1", "core3", "minor0", "n.T0", "et", "z3", "major2", "ert", "n.TE", "v4", "m.SE",
    "minor1", "major3", "m.T0", "minor2", "z4", "m.TE", "n.T1", "n.T2", "p.SE", "v5", "c.S0", "p.T0", "p.TE",
    "minor3", "n.T3", "m.T1", "m.T2", "z5", "c.SE", "c.TE", "c.T0", "g.SE", "g.S0", "v6", "c.S1", "p.T1", "m.T3",
    "g.TE", "lowtop", "g.T0", "uppers0", "p.T2", "z6", "lowers", "c.T1", "p.T3", "g.S1", "v7", "c.S2", "update0",
    "c.T2", "g.T1", "uppers1", "g.S2", "c.T3", "update1", "g.T2", "uppers2", "v8", "c.S3", "g.T3", "update2",
    "uppers3", "g.S3", "update3",
)
BIG = SIDE * 16
SHARD = 16
BF = jnp.bfloat16
F32 = jnp.float32


def dot(a, b):
    return jnp.dot(a, b, preferred_element_type=F32)


def turned(row):
    n = row.shape[1]
    i = lax.broadcasted_iota(jnp.int32, (n, n), 0)
    j = lax.broadcasted_iota(jnp.int32, (n, n), 1)
    return jnp.sum(jnp.where(i == j, row, 0), axis=1, keepdims=True)


def kernel(
    a_hbm, piv_hbm, li_hbm, ui_hbm, ap,
    a, t, su, ps, po, xr, r1, q, r2, w, dl, oh, keep, se, l0t, u0w, li, ui, piv_ref,
    load_sem, part_sem,
    x_ss, x_rs, r1_ss, r1_rs, r2_ss, r2_rs, v_ss, v_rs,
    g1_ss, g1_rs, g2_ss, g2_rs, c_ss, c_rs, z_ss, z_rs, e_ss, e_rs, q_ss, q_rs,
):
    row = lax.axis_index("row")
    z = lax.axis_index("col")
    core = lax.rem(row, 2)
    yy = lax.rem(row // 2, SIDE)
    xx = row // (2 * SIDE)
    m = jnp.where(core == 0, xx, yy)
    n = jnp.where(core == 0, yy, xx)

    def at(mm, nn):
        mm, nn = lax.rem(mm + SIDE, SIDE), lax.rem(nn + SIDE, SIDE)
        return (jnp.where(core == 0, mm * SIDE + nn, nn * SIDE + mm) * 2 + core, z)

    sibling = (row + 1 - 2 * core, z)

    def along(k):
        return (row, lax.rem(z + k + ZS, ZS))

    s = su.at[pl.ds(0, 2 * NB)]

    def send(src, dst, ss_, rs_, dev):
        return pltpu.make_async_remote_copy(
            src_ref=src, dst_ref=dst, send_sem=ss_, recv_sem=rs_, device_id=dev, device_id_type=MESH
        )

    def load_a(c):
        cc = pl.ds(STARTS[c], WIDTHS[c])
        return pltpu.make_async_copy(a_hbm.at[:, cc], a.at[:, cc], part_sem.at[c])

    load_l = pltpu.make_async_copy(li_hbm, li, load_sem.at[1])
    load_u = pltpu.make_async_copy(ui_hbm, ui, load_sem.at[2])
    load_p = pltpu.make_async_copy(piv_hbm, piv_ref, load_sem.at[3])
    load_p.start()
    for c in CHUNKS:
        load_a(c).start()
    load_l.start()
    load_u.start()

    barrier = pltpu.get_barrier_semaphore()
    partners = [sibling]
    partners += [at(m + k, n) for k in (1, 2, 3)]
    partners += [at(m, n + k) for k in (1, 2, 3)]
    partners += [along(k) for k in range(1, ZS)]
    for dev in partners:
        pl.semaphore_signal(barrier, inc=1, device_id=dev, device_id_type=MESH)

    root = (m == 0) & (n == 0)
    off_lines = (m != 0) & (n != 0)

    @pl.when(root)
    def _():
        for mm in range(1, SIDE):
            for nn in range(1, SIDE):
                pl.semaphore_signal(barrier, inc=1, device_id=at(mm, nn), device_id_type=MESH)

    @pl.when(off_lines)
    def _():
        pl.semaphore_signal(barrier, inc=1, device_id=at(0, 0), device_id_type=MESH)

    more = jnp.where(root, (SIDE - 1) * (SIDE - 1), 0) + jnp.where(off_lines, 1, 0)
    pl.semaphore_wait(barrier, len(partners) + more)

    mine = core * NB

    def z_copy(blk, b, to, way, first):
        rows = pl.ds(b * NB, NB)
        cols = pl.ds(blk * NB, NB)
        src = a_hbm.at[rows, pl.ds(0, NB)] if first else w.at[rows, cols]
        return send(src, w.at[rows, cols], z_ss.at[blk, b, way], z_rs.at[blk, b], along(to))

    def own_panel(blk):
        return pltpu.make_async_copy(a_hbm.at[:, pl.ds(0, NB)], w.at[:, pl.ds(blk * NB, NB)], load_sem.at[4])

    def z_start(blk):
        @pl.when(z == blk)
        def _():
            for b in range(ROWS // NB):
                z_copy(blk, b, 1, 0, True).start()
                z_copy(blk, b, -1, 1, True).start()
            own_panel(blk).start()

    def z_wave(wave):
        for blk in (1, 0):
            rel = lax.rem(z - blk + ZS, ZS)
            for b in range(ROWS // NB):
                hops = wave - b
                if 1 <= hops <= 3:

                    @pl.when(rel == hops)
                    def _():
                        z_copy(blk, b, 1, 0, False).wait_recv()
                        z_copy(blk, b, 1, 0, False).start()

                if 1 <= hops <= 2:

                    @pl.when(rel == ZS - hops)
                    def _():
                        z_copy(blk, b, 1, 0, False).wait_recv()
                        z_copy(blk, b, -1, 1, False).start()

    def z_last(blk):
        rel = lax.rem(z - blk + ZS, ZS)

        @pl.when((rel == 4) | (rel == 5))
        def _():
            for b in range(ROWS // NB):
                z_copy(blk, b, 1, 0, False).wait_recv()

    def z_end(blk):
        rel = lax.rem(z - blk + ZS, ZS)

        for b in range(ROWS // NB):

            @pl.when(rel <= 3)
            def _():
                z_copy(blk, b, 1, 0, False).wait_send()

            @pl.when((rel == 0) | (rel >= 6))
            def _():
                z_copy(blk, b, -1, 1, False).wait_send()

    root = (m == 0) & (n == 0)

    def shard(mm, nn):
        return pl.ds(pl.multiple_of(mine + mm * BIG + nn * SHARD, SHARD), SHARD)

    own_rows = pltpu.make_async_copy(
        a_hbm.at[pl.ds(0, NB)], su.at[pl.ds(pl.multiple_of(mine, NB), NB), pl.ds(0, COLS)], load_sem.at[5]
    )
    flip = 1 - 2 * core

    depths, passes, inner = [], [], []
    for sign in (1, -1):
        px = lax.rem(sign * m + SIDE, SIDE)
        py = lax.rem(sign * flip * n + SIDE, SIDE)
        depth = 0
        go = [False] * 4
        for x, y, way, h in TREE:
            depth = depth + jnp.where((px == x) & (py == y), h, 0)
            go[way] = go[way] | ((px == (x - STEP_X[way]) % SIDE) & (py == (y - STEP_Y[way]) % SIDE))
        depths.append(depth)
        inner.append(go[0] | go[1] | go[2] | go[3])
        passes.append(go)

    def v_copy(tree, b, way, first=False):
        sign = 1 - 2 * tree
        cols = pl.ds(S_STARTS[b], S_WIDTHS[b])
        dst = su.at[pl.ds(pl.multiple_of(mine + tree * HALF, HALF), HALF), cols]
        src = a_hbm.at[pl.ds(tree * HALF, HALF), cols] if first else dst
        to = at(m + sign * STEP_X[way], n + sign * flip * STEP_Y[way])
        return send(src, dst, v_ss.at[tree, b, way], v_rs.at[tree, b], to)

    def s_start():
        @pl.when(root)
        def _():
            own_rows.start()
            for b in S_CHUNKS:
                for tree in range(2):
                    v_copy(tree, b, 0, True).start()

    def s_wave(wave):
        for b in S_CHUNKS:
            hops = wave - b
            if not 1 <= hops <= DEPTH:
                continue
            for tree in range(2):

                @pl.when((depths[tree] == hops) & inner[tree])
                def _():
                    v_copy(tree, b, 0).wait_recv()
                    for way in range(4):
                        if any(h == hops + 1 and e == way for _, _, e, h in TREE):

                            @pl.when(passes[tree][way])
                            def _():
                                v_copy(tree, b, way).start()

        if wave == 1:

            @pl.when(root)
            def _():
                own_rows.wait()

    def s_leaf(b):
        for tree in range(2):

            @pl.when(jnp.logical_not(inner[tree]))
            def _():
                v_copy(tree, b, 0).wait_recv()

    def s_end():
        for tree in range(2):
            for b in S_CHUNKS:
                for way in range(4):

                    @pl.when(passes[tree][way])
                    def _():
                        v_copy(tree, b, way).wait_send()

    bufs = (t, s)

    def q_copy(i):
        mm, nn = (i + 1) // SIDE, (i + 1) % SIDE
        rows = pl.ds(mm * BIG + nn * SHARD, SHARD)
        return send(a_hbm.at[rows, pl.ds(0, NB)], se, q_ss.at[i], q_rs, at(mm, nn))

    own_shard = pltpu.make_async_copy(a_hbm.at[pl.ds(0, SHARD), pl.ds(0, NB)], se, load_sem.at[6])

    def q_start():
        @pl.when(root & (z < 2))
        def _():
            for i in range(SIDE * SIDE - 1):
                q_copy(i).start()
            own_shard.start()

    def q_wait():
        @pl.when(jnp.logical_not(root) & (z < 2))
        def _():
            q_copy(0).wait_recv()

        @pl.when(root & (z < 2))
        def _():
            own_shard.wait()

    def q_end():
        @pl.when(root & (z < 2))
        def _():
            for i in range(SIDE * SIDE - 1):
                q_copy(i).wait_send()

    def e_copy(kind, blk, k):
        rows = shard(m, n)
        buf = bufs[kind]
        to = COLS + blk * NB if kind else COLS
        src = se if kind else buf.at[rows, pl.ds(0, NB)]
        return send(
            src, buf.at[rows, pl.ds(to, NB)], e_ss.at[kind, k - 1], e_rs.at[kind, blk], along(k)
        )

    def e_sources(kind):
        return ((0, z == 0), (1, z == 1)) if kind else ((0, z == 1 - core),)

    def e_start(kind):
        if kind:
            q_wait()
        for blk, here in e_sources(kind):

            @pl.when(here)
            def _():
                for k in (4, 3, 5, 2, 6, 1, 7):
                    e_copy(kind, blk, k).start()
                to = COLS + blk * NB if kind else COLS
                bufs[kind][shard(m, n), to : to + NB] = se[...] if kind else t[shard(m, n), 0:NB]

    def e_recv(kind):
        for blk, here in e_sources(kind):

            @pl.when(jnp.logical_not(here))
            def _():
                e_copy(kind, blk, 1).wait_recv()

    def e_end(kind):
        for blk, here in e_sources(kind):

            @pl.when(here)
            def _():
                for k in range(1, ZS):
                    e_copy(kind, blk, k).wait_send()

    def cols_of(c):
        return pl.ds(STARTS[c], WIDTHS[c])

    def x_copy(c):
        return send(ps.at[:, cols_of(c)], xr.at[:, cols_of(c)], x_ss.at[c], x_rs.at[c], sibling)

    def picks(c):
        load_a(c).wait()

        def body(i, carry):
            cc = pl.ds(pl.multiple_of(STARTS[c] + i * NB, NB), NB)
            both = dot(oh[...], a[:, cc]).astype(BF)
            ps[:, cc] = both[0:NB]
            po[:, cc] = both[NB : 2 * NB]
            return carry

        lax.fori_loop(0, WIDTHS[c] // NB, body, 0)
        x_copy(c).start()

    def r1_copy(c, k):
        g = lax.rem(m + k, SIDE)
        return send(
            po.at[pl.ds(pl.multiple_of(g * BIG, BIG), BIG), cols_of(c)], r1.at[k - 1, :, cols_of(c)],
            r1_ss.at[c, k - 1], r1_rs.at[c, k - 1], at(m + k, n),
        )

    def reduce_core(c):
        x_copy(c).wait_recv()
        po[:, cols_of(c)] = po[:, cols_of(c)] + xr[:, cols_of(c)]
        for k in (2, 1, 3):
            r1_copy(c, k).start()

    def r2_copy(c, k):
        g = lax.rem(n + k, SIDE)
        return send(
            q.at[pl.ds(pl.multiple_of(g * SHARD, SHARD), SHARD), cols_of(c)], r2.at[k - 1, :, cols_of(c)],
            r2_ss.at[c, k - 1], r2_rs.at[c, k - 1], at(m, n + k),
        )

    def reduce_major(c):
        for k in (1, 3, 2):
            r1_copy(c, k).wait_recv()
        cc = cols_of(c)
        own = po[pl.ds(pl.multiple_of(m * BIG, BIG), BIG), cc]
        q[:, cc] = (own + r1[0, :, cc]) + (r1[1, :, cc] + r1[2, :, cc])
        for k in (2, 1, 3):
            r2_copy(c, k).start()

    def reduce_minor(c):
        for k in (1, 3, 2):
            r2_copy(c, k).wait_recv()
        cc = cols_of(c)
        own = q[pl.ds(pl.multiple_of(n * SHARD, SHARD), SHARD), cc]
        t[shard(m, n), cc] = (own + r2[0, :, cc]) + (r2[1, :, cc] + r2[2, :, cc])

    items = [(1, S_STARTS[c], S_WIDTHS[c]) for c in S_CHUNKS] + [(1, COLS, 2 * NB), (0, COLS, NB)]
    items += [(0, STARTS[c], WIDTHS[c]) for c in CHUNKS]

    def g1_copy(i, k):
        kind, c0, width = items[i]
        part = bufs[kind].at[shard(m, n), pl.ds(c0, width)]
        return send(part, part, g1_ss.at[i, k - 1], g1_rs.at[i, k - 1], at(m, n + k))

    def gather_minor(i):
        for k in (2, 1, 3):
            g1_copy(i, k).start()

    def block(mm):
        return pl.ds(pl.multiple_of(mine + lax.rem(mm + SIDE, SIDE) * BIG, BIG), BIG)

    ways = ((0, 0, 1), (0, 1, -1), (0, 1, 1), (0, 0, -1), (-1, 0, 1), (1, 1, -1))

    def g2_copy(i, j):
        kind, c0, width = items[i]
        who, half, way = ways[j]
        part = bufs[kind].at[block(m + who), pl.ds(c0 + half * (width // 2), width // 2)]
        return send(part, part, g2_ss.at[i, j], g2_rs.at[i, j], at(m + way, n))

    def gather_major(i):
        for k in (1, 3, 2):
            g1_copy(i, k).wait_recv()
        for j in range(4):
            g2_copy(i, j).start()

    def gather_pass(i):
        g2_copy(i, 0).wait_recv()
        g2_copy(i, 4).start()
        g2_copy(i, 1).wait_recv()
        g2_copy(i, 5).start()

    def c_copy(i):
        kind, c0, width = items[i]
        part = bufs[kind].at[pl.ds(pl.multiple_of(mine, NB), NB), pl.ds(c0, width)]
        return send(part, part, c_ss.at[i], c_rs.at[i], sibling)

    def gather_core(i):
        if i < len(S_WIDTHS):
            s_leaf(i)
        else:
            for j in (2, 3, 4, 5):
                g2_copy(i, j).wait_recv()
        c_copy(i).start()

    def gathered(i):
        c_copy(i).wait_recv()

    def lowtop():
        load_l.wait()
        load_u.wait()
        l0t[...] = dot(t[NB : 2 * NB, COLS : COLS + NB], ui[0]).astype(BF)
        u0w[...] = dot(li[0], t[0:NB, COLS : COLS + NB]).astype(BF)

    def lowers():
        for blk in range(2):
            z_last(blk)

            @pl.when(z == blk)
            def _():
                own_panel(blk).wait()

        def body(b, carry):
            rows = pl.ds(pl.multiple_of(b * NB, NB), NB)
            stay = jnp.concatenate([keep[rows, :], keep[rows, :]], axis=1) > 0.5
            take = dl[rows, 0 : 2 * NB]
            w0 = jnp.where(stay, w[rows, 0:NB].astype(F32), dot(take, s[:, COLS : COLS + NB])).astype(BF)
            w1 = jnp.where(stay, w[rows, NB : 2 * NB].astype(F32), dot(take, s[:, COLS + NB : COLS + 2 * NB]))
            low0 = dot(w0, ui[0]).astype(BF)
            x1 = (w1 - dot(low0, u0w[...])).astype(BF)
            dl[rows, 2 * NB : 3 * NB] = -low0
            dl[rows, 3 * NB : 4 * NB] = -dot(x1, ui[1]).astype(BF)
            return carry

        lax.fori_loop(0, ROWS // NB, body, 0)

    def uppers(c):
        cc = cols_of(c)
        u0 = dot(li[0], t[0:NB, cc]).astype(BF)
        su[2 * NB : 3 * NB, cc] = u0
        x1 = (t[NB : 2 * NB, cc].astype(F32) - dot(l0t[...], u0)).astype(BF)
        su[3 * NB : 4 * NB, cc] = dot(li[1], x1).astype(BF)

    def update(c):
        def body(i, carry):
            cc = pl.ds(pl.multiple_of(S_STARTS[c] + i * NB, NB), NB)
            stay = jnp.concatenate([keep[...], keep[...]], axis=1) > 0.5
            base = jnp.where(stay, a[:, cc].astype(F32), 0.0)
            ap[:, cc] = (base + dot(dl[...], su[:, cc])).astype(BF)
            return carry

        lax.fori_loop(0, S_WIDTHS[c] // NB, body, 0)
        cc = pl.ds(S_STARTS[c], S_WIDTHS[c])

        @pl.when(row == 0)
        def _():
            ap[0:NB, cc] = su[2 * NB : 3 * NB, cc]

        @pl.when(row == 1)
        def _():
            ap[0:NB, cc] = su[3 * NB : 4 * NB, cc]

        if c == 0:
            panel_out()

    def panel_out():
        @pl.when((z == 0) & (row > 0))
        def _():
            ap[0:NB, 0:NB] = -dl[0:NB, 2 * NB : 3 * NB]

        @pl.when((z == 1) & (row > 1))
        def _():
            ap[0:NB, 0:NB] = -dl[0:NB, 3 * NB : 4 * NB]

        @pl.when(z == 0)
        def _():
            ap[NB:ROWS, 0:NB] = -dl[NB:ROWS, 2 * NB : 3 * NB]

        @pl.when(z == 1)
        def _():
            ap[NB:ROWS, 0:NB] = -dl[NB:ROWS, 3 * NB : 4 * NB]

        @pl.when((z == 0) & (row == 0))
        def _():
            ap[0:NB, 0:NB] = t[0:NB, 0:NB]

        @pl.when((z == 0) & (row == 1))
        def _():
            ap[0:NB, 0:NB] = l0t[...]

        @pl.when((z == 1) & (row == 1))
        def _():
            ap[0:NB, 0:NB] = (t[NB : 2 * NB, 0:NB].astype(F32) - dot(l0t[...], u0w[...])).astype(BF)

    q_start()
    s_start()
    z_start(0)
    z_start(1)

    load_p.wait()
    p0r, p1r = piv_ref[0:1, :], piv_ref[1:2, :]
    p0c, p1c = turned(p0r), turned(p1r)
    i0 = lax.broadcasted_iota(jnp.int32, (NB, NB), 0)
    i1 = lax.broadcasted_iota(jnp.int32, (NB, NB), 1)
    hit = p1c == p0r
    src1 = jnp.where(
        jnp.max(hit.astype(jnp.int32), axis=1, keepdims=True) > 0,
        jnp.sum(jnp.where(hit, i1, 0), axis=1, keepdims=True),
        p1c,
    )
    src_other = jnp.where(core == 0, src1, p0c)
    src_mine = jnp.where(core == 0, p0c, src1)
    for b in range(ROWS // NB):
        glob_r = b * (NB * 2 * SIDE * SIDE) + row * NB + i1
        oh[0:NB, b * NB : (b + 1) * NB] = (src_other == glob_r).astype(F32).astype(BF)
        oh[NB : 2 * NB, b * NB : (b + 1) * NB] = (src_mine == glob_r).astype(F32).astype(BF)

    def places():
        hit_top = p0r == NB + i0
        out_in = jnp.sum(jnp.where(hit_top, p1c, 0), axis=0, keepdims=True)
        met = jnp.max(hit.astype(jnp.int32), axis=0, keepdims=True) > 0
        met_at = jnp.sum(jnp.where(hit, NB + i0, 0), axis=0, keepdims=True)
        dest0 = jnp.where(p0r < NB, p0r, jnp.where(p0r < 2 * NB, out_in, jnp.where(met, met_at, p0r)))
        back = p0c == NB + i1
        dest1 = jnp.where(
            jnp.max(back.astype(jnp.int32), axis=0, keepdims=True) > 0,
            jnp.sum(jnp.where(back, i0, 0), axis=0, keepdims=True),
            p1r,
        )
        for b in range(ROWS // NB):
            rows = pl.ds(b * NB, NB)
            glob_c = b * (NB * 2 * SIDE * SIDE) + row * NB + i0
            d0 = dest0 == glob_c
            d1 = dest1 == glob_c
            dl[rows, 0:NB] = d0.astype(F32).astype(BF)
            dl[rows, NB : 2 * NB] = d1.astype(F32).astype(BF)
            moved = jnp.max(jnp.maximum(d0.astype(F32), d1.astype(F32)), axis=1, keepdims=True)
            keep[rows, :] = jnp.broadcast_to(1.0 - moved, (NB, 128))

    names = ["S%d" % c for c in S_CHUNKS] + ["SE", "TE"] + ["T%d" % c for c in CHUNKS]
    gathers = {"n": gather_minor, "m": gather_major, "p": gather_pass, "c": gather_core, "g": gathered}
    stages = {
        "picks": picks, "core": reduce_core, "major": reduce_major, "minor": reduce_minor,
        "uppers": uppers, "update": update, "z": z_wave, "v": s_wave,
    }
    single = {
        "et": (e_start, 0), "es": (e_start, 1), "ert": (e_recv, 0), "ers": (e_recv, 1),
        "lowers": (lowers,), "lowtop": (lowtop,), "places": (places,),
    }
    steps = []
    for word in PLAN:
        if "." in word:
            steps.append((gathers[word[0]], names.index(word[2:])))
        elif word in single:
            steps.append(single[word])
        else:
            steps.append((stages[word[:-1]], int(word[-1])))
    for step, *which in steps:
        step(*which)

    q_end()
    s_end()
    z_end(0)
    z_end(1)
    e_end(0)
    e_end(1)
    for c in CHUNKS:
        x_copy(c).wait_send()
        for k in (1, 2, 3):
            r1_copy(c, k).wait_send()
            r2_copy(c, k).wait_send()
    for i in range(len(items)):
        c_copy(i).wait_send()
    for i in range(len(S_WIDTHS), len(items)):
        for k in (1, 2, 3):
            g1_copy(i, k).wait_send()
        for j in range(6):
            g2_copy(i, j).wait_send()


def per_device(a_stored, pivots, l_inverse, u_inverse):
    chunks = len(WIDTHS)
    n_items = 2 + chunks + len(S_WIDTHS)
    dma = pltpu.SemaphoreType.DMA
    hbm = pl.BlockSpec(memory_space=pltpu.HBM)
    scratch = [
        pltpu.VMEM((ROWS, COLS), BF),
        pltpu.VMEM((2 * NB, COLS + NB), BF),
        pltpu.VMEM((4 * NB, COLS + 2 * NB), BF),
        pltpu.VMEM((NB, COLS), BF),
        pltpu.VMEM((NB, COLS), BF),
        pltpu.VMEM((NB, COLS), BF),
        pltpu.VMEM((3, BIG, COLS), BF),
        pltpu.VMEM((BIG, COLS), BF),
        pltpu.VMEM((3, SHARD, COLS), BF),
        pltpu.VMEM((ROWS, 2 * NB), BF),
        pltpu.VMEM((ROWS, 4 * NB), BF),
        pltpu.VMEM((2 * NB, ROWS), BF),
        pltpu.VMEM((ROWS, 128), F32),
        pltpu.VMEM((SHARD, NB), BF),
        pltpu.VMEM((NB, NB), BF),
        pltpu.VMEM((NB, NB), BF),
        pltpu.VMEM((2, NB, NB), BF),
        pltpu.VMEM((2, NB, NB), BF),
        pltpu.VMEM((2, NB), jnp.int32),
        dma((7,)), dma((chunks,)),
        dma((chunks,)), dma((chunks,)),
        dma((chunks, 3)), dma((chunks, 3)),
        dma((chunks, 3)), dma((chunks, 3)),
        dma((2, len(S_WIDTHS), 4)), dma((2, len(S_WIDTHS))),
        dma((n_items, 3)), dma((n_items, 3)),
        dma((n_items, 6)), dma((n_items, 6)),
        dma((n_items,)), dma((n_items,)),
        dma((2, 3, 2)), dma((2, 3)),
        dma((2, ZS - 1)), dma((2, 2)),
        dma((SIDE * SIDE - 1,)), dma,
    ]
    return pl.pallas_call(
        kernel,
        out_shape=jax.ShapeDtypeStruct((ROWS, COLS), BF),
        in_specs=[hbm] * 4,
        out_specs=pl.BlockSpec(memory_space=pltpu.VMEM),
        scratch_shapes=scratch,
        compiler_params=pltpu.CompilerParams(
            collective_id=0, has_side_effects=True, vmem_limit_bytes=48 * 2**20
        ),
        name="panels",
    )(a_stored, pivots, l_inverse, u_inverse)


def solution(mesh):
    in_specs = (P("row", "col"), P(), P(), P())
    out_specs = P("row", "col")
    return jax.shard_map(
        per_device, mesh=mesh, in_specs=in_specs, out_specs=out_specs, check_vma=False
    )
```

```python
import functools

import jax
import jax.numpy as jnp
from jax import lax
from jax.experimental import pallas as pl
from jax.experimental.pallas import tpu as pltpu
from jax.sharding import PartitionSpec as P

MESH = pl.DeviceIdType.MESH
NB = 256
SIDE = 4
ZS = 8
ROWS, COLS = 768, 3072
WIDTHS = (768, 768, 768, 768)
STARTS = tuple(sum(WIDTHS[:c]) for c in range(len(WIDTHS)))
CHUNKS = range(len(WIDTHS))
S_WIDTHS = (768, 768, 768, 768)
S_STARTS = tuple(sum(S_WIDTHS[:c]) for c in range(len(S_WIDTHS)))
S_CHUNKS = range(len(S_WIDTHS))
TREE = (
    (1, 0, 0, 1), (1, 1, 1, 2), (1, 3, 3, 2), (2, 0, 0, 2), (0, 1, 2, 3), (0, 3, 2, 3), (1, 2, 3, 3), (2, 1, 1, 3),
    (2, 3, 0, 3), (3, 0, 0, 3), (0, 2, 2, 4), (2, 2, 1, 4), (3, 1, 0, 4), (3, 3, 0, 4), (3, 2, 0, 5),
)
DEPTH = 5
STEP_X, STEP_Y = (1, 0, -1, 0), (0, 1, 0, -1)
HALF = NB // 2
PLAN = (
    "picks0", "v1", "picks1", "z1", "es", "core0", "picks2", "v2", "core1", "picks3", "places", "z2", "ers", "n.SE",
    "major0", "core2", "v3", "major1", "core3", "minor0", "n.T0", "et", "z3", "major2", "ert", "n.TE", "v4", "m.SE",
    "minor1", "major3", "m.T0", "minor2", "z4", "m.TE", "n.T1", "n.T2", "p.SE", "v5", "c.S0", "p.T0", "p.TE",
    "minor3", "n.T3", "m.T1", "m.T2", "z5", "c.SE", "c.TE", "c.T0", "g.SE", "g.S0", "v6", "c.S1", "p.T1", "m.T3",
    "g.TE", "lowtop", "g.T0", "uppers0", "p.T2", "z6", "lowers", "c.T1", "p.T3", "g.S1", "v7", "c.S2", "update0",
    "c.T2", "g.T1", "uppers1", "g.S2", "c.T3", "update1", "g.T2", "uppers2", "v8", "c.S3", "g.T3", "update2",
    "uppers3", "g.S3", "update3",
)
BIG = SIDE * 16
SHARD = 16
BF = jnp.bfloat16
F32 = jnp.float32


def dot(a, b):
    return jnp.dot(a, b, preferred_element_type=F32)


def turned(row):
    n = row.shape[1]
    i = lax.broadcasted_iota(jnp.int32, (n, n), 0)
    j = lax.broadcasted_iota(jnp.int32, (n, n), 1)
    return jnp.sum(jnp.where(i == j, row, 0), axis=1, keepdims=True)


def kernel(
    a_hbm, piv_hbm, li_hbm, ui_hbm, ap,
    a, t, su, ps, po, xr, r1, q, r2, w, dl, oh, keep, se, l0t, u0w, li, ui, piv_ref,
    load_sem, part_sem,
    x_ss, x_rs, r1_ss, r1_rs, r2_ss, r2_rs, v_ss, v_rs,
    g1_ss, g1_rs, g2_ss, g2_rs, c_ss, c_rs, z_ss, z_rs, e_ss, e_rs, q_ss, q_rs,
):
    row = lax.axis_index("row")
    z = lax.axis_index("col")
    core = lax.rem(row, 2)
    yy = lax.rem(row // 2, SIDE)
    xx = row // (2 * SIDE)
    m = jnp.where(core == 0, xx, yy)
    n = jnp.where(core == 0, yy, xx)

    def at(mm, nn):
        mm, nn = lax.rem(mm + SIDE, SIDE), lax.rem(nn + SIDE, SIDE)
        return (jnp.where(core == 0, mm * SIDE + nn, nn * SIDE + mm) * 2 + core, z)

    sibling = (row + 1 - 2 * core, z)

    def along(k):
        return (row, lax.rem(z + k + ZS, ZS))

    s = su.at[pl.ds(0, 2 * NB)]

    def send(src, dst, ss_, rs_, dev):
        return pltpu.make_async_remote_copy(
            src_ref=src, dst_ref=dst, send_sem=ss_, recv_sem=rs_, device_id=dev, device_id_type=MESH
        )

    def load_a(c):
        cc = pl.ds(STARTS[c], WIDTHS[c])
        return pltpu.make_async_copy(a_hbm.at[:, cc], a.at[:, cc], part_sem.at[c])

    load_l = pltpu.make_async_copy(li_hbm, li, load_sem.at[1])
    load_u = pltpu.make_async_copy(ui_hbm, ui, load_sem.at[2])
    load_p = pltpu.make_async_copy(piv_hbm, piv_ref, load_sem.at[3])
    load_p.start()
    for c in CHUNKS:
        load_a(c).start()
    load_l.start()
    load_u.start()

    barrier = pltpu.get_barrier_semaphore()
    partners = [sibling]
    partners += [at(m + k, n) for k in (1, 2, 3)]
    partners += [at(m, n + k) for k in (1, 2, 3)]
    partners += [along(k) for k in range(1, ZS)]
    for dev in partners:
        pl.semaphore_signal(barrier, inc=1, device_id=dev, device_id_type=MESH)

    root = (m == 0) & (n == 0)
    off_lines = (m != 0) & (n != 0)

    @pl.when(root)
    def _():
        for mm in range(1, SIDE):
            for nn in range(1, SIDE):
                pl.semaphore_signal(barrier, inc=1, device_id=at(mm, nn), device_id_type=MESH)

    @pl.when(off_lines)
    def _():
        pl.semaphore_signal(barrier, inc=1, device_id=at(0, 0), device_id_type=MESH)

    more = jnp.where(root, (SIDE - 1) * (SIDE - 1), 0) + jnp.where(off_lines, 1, 0)
    pl.semaphore_wait(barrier, len(partners) + more)

    mine = core * NB

    def z_copy(blk, b, to, way, first):
        rows = pl.ds(b * NB, NB)
        cols = pl.ds(blk * NB, NB)
        src = a_hbm.at[rows, pl.ds(0, NB)] if first else w.at[rows, cols]
        return send(src, w.at[rows, cols], z_ss.at[blk, b, way], z_rs.at[blk, b], along(to))

    def own_panel(blk):
        return pltpu.make_async_copy(a_hbm.at[:, pl.ds(0, NB)], w.at[:, pl.ds(blk * NB, NB)], load_sem.at[4])

    def z_start(blk):
        @pl.when(z == blk)
        def _():
            for b in range(ROWS // NB):
                z_copy(blk, b, 1, 0, True).start()
                z_copy(blk, b, -1, 1, True).start()
            own_panel(blk).start()

    def z_wave(wave):
        for blk in (1, 0):
            rel = lax.rem(z - blk + ZS, ZS)
            for b in range(ROWS // NB):
                hops = wave - b
                if 1 <= hops <= 3:

                    @pl.when(rel == hops)
                    def _():
                        z_copy(blk, b, 1, 0, False).wait_recv()
                        z_copy(blk, b, 1, 0, False).start()

                if 1 <= hops <= 2:

                    @pl.when(rel == ZS - hops)
                    def _():
                        z_copy(blk, b, 1, 0, False).wait_recv()
                        z_copy(blk, b, -1, 1, False).start()

    def z_last(blk):
        rel = lax.rem(z - blk + ZS, ZS)

        @pl.when((rel == 4) | (rel == 5))
        def _():
            for b in range(ROWS // NB):
                z_copy(blk, b, 1, 0, False).wait_recv()

    def z_end(blk):
        rel = lax.rem(z - blk + ZS, ZS)

        for b in range(ROWS // NB):

            @pl.when(rel <= 3)
            def _():
                z_copy(blk, b, 1, 0, False).wait_send()

            @pl.when((rel == 0) | (rel >= 6))
            def _():
                z_copy(blk, b, -1, 1, False).wait_send()

    root = (m == 0) & (n == 0)

    def shard(mm, nn):
        return pl.ds(pl.multiple_of(mine + mm * BIG + nn * SHARD, SHARD), SHARD)

    own_rows = pltpu.make_async_copy(
        a_hbm.at[pl.ds(0, NB)], su.at[pl.ds(pl.multiple_of(mine, NB), NB), pl.ds(0, COLS)], load_sem.at[5]
    )
    flip = 1 - 2 * core

    depths, passes, inner = [], [], []
    for sign in (1, -1):
        px = lax.rem(sign * m + SIDE, SIDE)
        py = lax.rem(sign * flip * n + SIDE, SIDE)
        depth = 0
        go = [False] * 4
        for x, y, way, h in TREE:
            depth = depth + jnp.where((px == x) & (py == y), h, 0)
            go[way] = go[way] | ((px == (x - STEP_X[way]) % SIDE) & (py == (y - STEP_Y[way]) % SIDE))
        depths.append(depth)
        inner.append(go[0] | go[1] | go[2] | go[3])
        passes.append(go)

    def v_copy(tree, b, way, first=False):
        sign = 1 - 2 * tree
        cols = pl.ds(S_STARTS[b], S_WIDTHS[b])
        dst = su.at[pl.ds(pl.multiple_of(mine + tree * HALF, HALF), HALF), cols]
        src = a_hbm.at[pl.ds(tree * HALF, HALF), cols] if first else dst
        to = at(m + sign * STEP_X[way], n + sign * flip * STEP_Y[way])
        return send(src, dst, v_ss.at[tree, b, way], v_rs.at[tree, b], to)

    def s_start():
        @pl.when(root)
        def _():
            own_rows.start()
            for b in S_CHUNKS:
                for tree in range(2):
                    v_copy(tree, b, 0, True).start()

    def s_wave(wave):
        for b in S_CHUNKS:
            hops = wave - b
            if not 1 <= hops <= DEPTH:
                continue
            for tree in range(2):

                @pl.when((depths[tree] == hops) & inner[tree])
                def _():
                    v_copy(tree, b, 0).wait_recv()
                    for way in range(4):
                        if any(h == hops + 1 and e == way for _, _, e, h in TREE):

                            @pl.when(passes[tree][way])
                            def _():
                                v_copy(tree, b, way).start()

        if wave == 1:

            @pl.when(root)
            def _():
                own_rows.wait()

    def s_leaf(b):
        for tree in range(2):

            @pl.when(jnp.logical_not(inner[tree]))
            def _():
                v_copy(tree, b, 0).wait_recv()

    def s_end():
        for tree in range(2):
            for b in S_CHUNKS:
                for way in range(4):

                    @pl.when(passes[tree][way])
                    def _():
                        v_copy(tree, b, way).wait_send()

    bufs = (t, s)

    def q_copy(i):
        mm, nn = (i + 1) // SIDE, (i + 1) % SIDE
        rows = pl.ds(mm * BIG + nn * SHARD, SHARD)
        return send(a_hbm.at[rows, pl.ds(0, NB)], se, q_ss.at[i], q_rs, at(mm, nn))

    own_shard = pltpu.make_async_copy(a_hbm.at[pl.ds(0, SHARD), pl.ds(0, NB)], se, load_sem.at[6])

    def q_start():
        @pl.when(root & (z < 2))
        def _():
            for i in range(SIDE * SIDE - 1):
                q_copy(i).start()
            own_shard.start()

    def q_wait():
        @pl.when(jnp.logical_not(root) & (z < 2))
        def _():
            q_copy(0).wait_recv()

        @pl.when(root & (z < 2))
        def _():
            own_shard.wait()

    def q_end():
        @pl.when(root & (z < 2))
        def _():
            for i in range(SIDE * SIDE - 1):
                q_copy(i).wait_send()

    def e_copy(kind, blk, k):
        rows = shard(m, n)
        buf = bufs[kind]
        to = COLS + blk * NB if kind else COLS
        src = se if kind else buf.at[rows, pl.ds(0, NB)]
        return send(
            src, buf.at[rows, pl.ds(to, NB)], e_ss.at[kind, k - 1], e_rs.at[kind, blk], along(k)
        )

    def e_sources(kind):
        return ((0, z == 0), (1, z == 1)) if kind else ((0, z == 1 - core),)

    def e_start(kind):
        if kind:
            q_wait()
        for blk, here in e_sources(kind):

            @pl.when(here)
            def _():
                for k in (4, 3, 5, 2, 6, 1, 7):
                    e_copy(kind, blk, k).start()
                to = COLS + blk * NB if kind else COLS
                bufs[kind][shard(m, n), to : to + NB] = se[...] if kind else t[shard(m, n), 0:NB]

    def e_recv(kind):
        for blk, here in e_sources(kind):

            @pl.when(jnp.logical_not(here))
            def _():
                e_copy(kind, blk, 1).wait_recv()

    def e_end(kind):
        for blk, here in e_sources(kind):

            @pl.when(here)
            def _():
                for k in range(1, ZS):
                    e_copy(kind, blk, k).wait_send()

    def cols_of(c):
        return pl.ds(STARTS[c], WIDTHS[c])

    def x_copy(c):
        return send(ps.at[:, cols_of(c)], xr.at[:, cols_of(c)], x_ss.at[c], x_rs.at[c], sibling)

    def picks(c):
        load_a(c).wait()

        def body(i, carry):
            cc = pl.ds(pl.multiple_of(STARTS[c] + i * NB, NB), NB)
            both = dot(oh[...], a[:, cc]).astype(BF)
            ps[:, cc] = both[0:NB]
            po[:, cc] = both[NB : 2 * NB]
            return carry

        lax.fori_loop(0, WIDTHS[c] // NB, body, 0)
        x_copy(c).start()

    def r1_copy(c, k):
        g = lax.rem(m + k, SIDE)
        return send(
            po.at[pl.ds(pl.multiple_of(g * BIG, BIG), BIG), cols_of(c)], r1.at[k - 1, :, cols_of(c)],
            r1_ss.at[c, k - 1], r1_rs.at[c, k - 1], at(m + k, n),
        )

    def reduce_core(c):
        x_copy(c).wait_recv()
        po[:, cols_of(c)] = po[:, cols_of(c)] + xr[:, cols_of(c)]
        for k in (2, 1, 3):
            r1_copy(c, k).start()

    def r2_copy(c, k):
        g = lax.rem(n + k, SIDE)
        return send(
            q.at[pl.ds(pl.multiple_of(g * SHARD, SHARD), SHARD), cols_of(c)], r2.at[k - 1, :, cols_of(c)],
            r2_ss.at[c, k - 1], r2_rs.at[c, k - 1], at(m, n + k),
        )

    def reduce_major(c):
        for k in (1, 3, 2):
            r1_copy(c, k).wait_recv()
        cc = cols_of(c)
        own = po[pl.ds(pl.multiple_of(m * BIG, BIG), BIG), cc]
        q[:, cc] = (own + r1[0, :, cc]) + (r1[1, :, cc] + r1[2, :, cc])
        for k in (2, 1, 3):
            r2_copy(c, k).start()

    def reduce_minor(c):
        for k in (1, 3, 2):
            r2_copy(c, k).wait_recv()
        cc = cols_of(c)
        own = q[pl.ds(pl.multiple_of(n * SHARD, SHARD), SHARD), cc]
        t[shard(m, n), cc] = (own + r2[0, :, cc]) + (r2[1, :, cc] + r2[2, :, cc])

    items = [(1, S_STARTS[c], S_WIDTHS[c]) for c in S_CHUNKS] + [(1, COLS, 2 * NB), (0, COLS, NB)]
    items += [(0, STARTS[c], WIDTHS[c]) for c in CHUNKS]

    def g1_copy(i, k):
        kind, c0, width = items[i]
        part = bufs[kind].at[shard(m, n), pl.ds(c0, width)]
        return send(part, part, g1_ss.at[i, k - 1], g1_rs.at[i, k - 1], at(m, n + k))

    def gather_minor(i):
        for k in (2, 1, 3):
            g1_copy(i, k).start()

    def block(mm):
        return pl.ds(pl.multiple_of(mine + lax.rem(mm + SIDE, SIDE) * BIG, BIG), BIG)

    ways = ((0, 0, 1), (0, 1, -1), (0, 1, 1), (0, 0, -1), (-1, 0, 1), (1, 1, -1))

    def g2_copy(i, j):
        kind, c0, width = items[i]
        who, half, way = ways[j]
        part = bufs[kind].at[block(m + who), pl.ds(c0 + half * (width // 2), width // 2)]
        return send(part, part, g2_ss.at[i, j], g2_rs.at[i, j], at(m + way, n))

    def gather_major(i):
        for k in (1, 3, 2):
            g1_copy(i, k).wait_recv()
        for j in range(4):
            g2_copy(i, j).start()

    def gather_pass(i):
        g2_copy(i, 0).wait_recv()
        g2_copy(i, 4).start()
        g2_copy(i, 1).wait_recv()
        g2_copy(i, 5).start()

    def c_copy(i):
        kind, c0, width = items[i]
        part = bufs[kind].at[pl.ds(pl.multiple_of(mine, NB), NB), pl.ds(c0, width)]
        return send(part, part, c_ss.at[i], c_rs.at[i], sibling)

    def gather_core(i):
        if i < len(S_WIDTHS):
            s_leaf(i)
        else:
            for j in (2, 3, 4, 5):
                g2_copy(i, j).wait_recv()
        c_copy(i).start()

    def gathered(i):
        c_copy(i).wait_recv()

    def lowtop():
        load_l.wait()
        load_u.wait()
        l0t[...] = dot(t[NB : 2 * NB, COLS : COLS + NB], ui[0]).astype(BF)
        u0w[...] = dot(li[0], t[0:NB, COLS : COLS + NB]).astype(BF)

    def lowers():
        for blk in range(2):
            z_last(blk)

            @pl.when(z == blk)
            def _():
                own_panel(blk).wait()

        def body(b, carry):
            rows = pl.ds(pl.multiple_of(b * NB, NB), NB)
            stay = jnp.concatenate([keep[rows, :], keep[rows, :]], axis=1) > 0.5
            take = dl[rows, 0 : 2 * NB]
            w0 = jnp.where(stay, w[rows, 0:NB].astype(F32), dot(take, s[:, COLS : COLS + NB])).astype(BF)
            w1 = jnp.where(stay, w[rows, NB : 2 * NB].astype(F32), dot(take, s[:, COLS + NB : COLS + 2 * NB]))
            low0 = dot(w0, ui[0]).astype(BF)
            x1 = (w1 - dot(low0, u0w[...])).astype(BF)
            dl[rows, 2 * NB : 3 * NB] = -low0
            dl[rows, 3 * NB : 4 * NB] = -dot(x1, ui[1]).astype(BF)
            return carry

        lax.fori_loop(0, ROWS // NB, body, 0)

    def uppers(c):
        cc = cols_of(c)
        u0 = dot(li[0], t[0:NB, cc]).astype(BF)
        su[2 * NB : 3 * NB, cc] = u0
        x1 = (t[NB : 2 * NB, cc].astype(F32) - dot(l0t[...], u0)).astype(BF)
        su[3 * NB : 4 * NB, cc] = dot(li[1], x1).astype(BF)

    def update(c):
        def body(i, carry):
            cc = pl.ds(pl.multiple_of(S_STARTS[c] + i * NB, NB), NB)
            stay = jnp.concatenate([keep[...], keep[...]], axis=1) > 0.5
            base = jnp.where(stay, a[:, cc].astype(F32), 0.0)
            ap[:, cc] = (base + dot(dl[...], su[:, cc])).astype(BF)
            return carry

        lax.fori_loop(0, S_WIDTHS[c] // NB, body, 0)
        cc = pl.ds(S_STARTS[c], S_WIDTHS[c])

        @pl.when(row == 0)
        def _():
            ap[0:NB, cc] = su[2 * NB : 3 * NB, cc]

        @pl.when(row == 1)
        def _():
            ap[0:NB, cc] = su[3 * NB : 4 * NB, cc]

        if c == 0:
            panel_out()

    def panel_out():
        @pl.when((z == 0) & (row > 0))
        def _():
            ap[0:NB, 0:NB] = -dl[0:NB, 2 * NB : 3 * NB]

        @pl.when((z == 1) & (row > 1))
        def _():
            ap[0:NB, 0:NB] = -dl[0:NB, 3 * NB : 4 * NB]

        @pl.when(z == 0)
        def _():
            ap[NB:ROWS, 0:NB] = -dl[NB:ROWS, 2 * NB : 3 * NB]

        @pl.when(z == 1)
        def _():
            ap[NB:ROWS, 0:NB] = -dl[NB:ROWS, 3 * NB : 4 * NB]

        @pl.when((z == 0) & (row == 0))
        def _():
            ap[0:NB, 0:NB] = t[0:NB, 0:NB]

        @pl.when((z == 0) & (row == 1))
        def _():
            ap[0:NB, 0:NB] = l0t[...]

        @pl.when((z == 1) & (row == 1))
        def _():
            ap[0:NB, 0:NB] = (t[NB : 2 * NB, 0:NB].astype(F32) - dot(l0t[...], u0w[...])).astype(BF)

    q_start()
    s_start()
    z_start(0)
    z_start(1)

    load_p.wait()
    p0r, p1r = piv_ref[0:1, :], piv_ref[1:2, :]
    p0c, p1c = turned(p0r), turned(p1r)
    i0 = lax.broadcasted_iota(jnp.int32, (NB, NB), 0)
    i1 = lax.broadcasted_iota(jnp.int32, (NB, NB), 1)
    hit = p1c == p0r
    src1 = jnp.where(
        jnp.max(hit.astype(jnp.int32), axis=1, keepdims=True) > 0,
        jnp.sum(jnp.where(hit, i1, 0), axis=1, keepdims=True),
        p1c,
    )
    src_other = jnp.where(core == 0, src1, p0c)
    src_mine = jnp.where(core == 0, p0c, src1)
    for b in range(ROWS // NB):
        glob_r = b * (NB * 2 * SIDE * SIDE) + row * NB + i1
        oh[0:NB, b * NB : (b + 1) * NB] = (src_other == glob_r).astype(F32).astype(BF)
        oh[NB : 2 * NB, b * NB : (b + 1) * NB] = (src_mine == glob_r).astype(F32).astype(BF)

    def places():
        hit_top = p0r == NB + i0
        out_in = jnp.sum(jnp.where(hit_top, p1c, 0), axis=0, keepdims=True)
        met = jnp.max(hit.astype(jnp.int32), axis=0, keepdims=True) > 0
        met_at = jnp.sum(jnp.where(hit, NB + i0, 0), axis=0, keepdims=True)
        dest0 = jnp.where(p0r < NB, p0r, jnp.where(p0r < 2 * NB, out_in, jnp.where(met, met_at, p0r)))
        back = p0c == NB + i1
        dest1 = jnp.where(
            jnp.max(back.astype(jnp.int32), axis=0, keepdims=True) > 0,
            jnp.sum(jnp.where(back, i0, 0), axis=0, keepdims=True),
            p1r,
        )
        for b in range(ROWS // NB):
            rows = pl.ds(b * NB, NB)
            glob_c = b * (NB * 2 * SIDE * SIDE) + row * NB + i0
            d0 = dest0 == glob_c
            d1 = dest1 == glob_c
            dl[rows, 0:NB] = d0.astype(F32).astype(BF)
            dl[rows, NB : 2 * NB] = d1.astype(F32).astype(BF)
            moved = jnp.max(jnp.maximum(d0.astype(F32), d1.astype(F32)), axis=1, keepdims=True)
            keep[rows, :] = jnp.broadcast_to(1.0 - moved, (NB, 128))

    names = ["S%d" % c for c in S_CHUNKS] + ["SE", "TE"] + ["T%d" % c for c in CHUNKS]
    gathers = {"n": gather_minor, "m": gather_major, "p": gather_pass, "c": gather_core, "g": gathered}
    stages = {
        "picks": picks, "core": reduce_core, "major": reduce_major, "minor": reduce_minor,
        "uppers": uppers, "update": update, "z": z_wave, "v": s_wave,
    }
    single = {
        "et": (e_start, 0), "es": (e_start, 1), "ert": (e_recv, 0), "ers": (e_recv, 1),
        "lowers": (lowers,), "lowtop": (lowtop,), "places": (places,),
    }
    steps = []
    for word in PLAN:
        if "." in word:
            steps.append((gathers[word[0]], names.index(word[2:])))
        elif word in single:
            steps.append(single[word])
        else:
            steps.append((stages[word[:-1]], int(word[-1])))
    for step, *which in steps:
        step(*which)

    q_end()
    s_end()
    z_end(0)
    z_end(1)
    e_end(0)
    e_end(1)
    for c in CHUNKS:
        x_copy(c).wait_send()
        for k in (1, 2, 3):
            r1_copy(c, k).wait_send()
            r2_copy(c, k).wait_send()
    for i in range(len(items)):
        c_copy(i).wait_send()
    for i in range(len(S_WIDTHS), len(items)):
        for k in (1, 2, 3):
            g1_copy(i, k).wait_send()
        for j in range(6):
            g2_copy(i, j).wait_send()


def per_device(a_stored, pivots, l_inverse, u_inverse):
    chunks = len(WIDTHS)
    n_items = 2 + chunks + len(S_WIDTHS)
    dma = pltpu.SemaphoreType.DMA
    hbm = pl.BlockSpec(memory_space=pltpu.HBM)
    scratch = [
        pltpu.VMEM((ROWS, COLS), BF),
        pltpu.VMEM((2 * NB, COLS + NB), BF),
        pltpu.VMEM((4 * NB, COLS + 2 * NB), BF),
        pltpu.VMEM((NB, COLS), BF),
        pltpu.VMEM((NB, COLS), BF),
        pltpu.VMEM((NB, COLS), BF),
        pltpu.VMEM((3, BIG, COLS), BF),
        pltpu.VMEM((BIG, COLS), BF),
        pltpu.VMEM((3, SHARD, COLS), BF),
        pltpu.VMEM((ROWS, 2 * NB), BF),
        pltpu.VMEM((ROWS, 4 * NB), BF),
        pltpu.VMEM((2 * NB, ROWS), BF),
        pltpu.VMEM((ROWS, 128), F32),
        pltpu.VMEM((SHARD, NB), BF),
        pltpu.VMEM((NB, NB), BF),
        pltpu.VMEM((NB, NB), BF),
        pltpu.VMEM((2, NB, NB), BF),
        pltpu.VMEM((2, NB, NB), BF),
        pltpu.VMEM((2, NB), jnp.int32),
        dma((7,)), dma((chunks,)),
        dma((chunks,)), dma((chunks,)),
        dma((chunks, 3)), dma((chunks, 3)),
        dma((chunks, 3)), dma((chunks, 3)),
        dma((2, len(S_WIDTHS), 4)), dma((2, len(S_WIDTHS))),
        dma((n_items, 3)), dma((n_items, 3)),
        dma((n_items, 6)), dma((n_items, 6)),
        dma((n_items,)), dma((n_items,)),
        dma((2, 3, 2)), dma((2, 3)),
        dma((2, ZS - 1)), dma((2, 2)),
        dma((SIDE * SIDE - 1,)), dma,
    ]
    small = [pltpu.with_memory_space_constraint(v, pltpu.HBM) for v in (pivots, l_inverse, u_inverse)]
    return pl.pallas_call(
        kernel,
        out_shape=jax.ShapeDtypeStruct((ROWS, COLS), BF),
        in_specs=[hbm] * 4,
        out_specs=pl.BlockSpec(memory_space=pltpu.VMEM),
        scratch_shapes=scratch,
        compiler_params=pltpu.CompilerParams(
            collective_id=0, has_side_effects=True, vmem_limit_bytes=48 * 2**20
        ),
        name="panels",
    )(a_stored, *small)


def solution(mesh):
    in_specs = (P("row", "col"), P(), P(), P())
    out_specs = P("row", "col")
    return jax.shard_map(
        per_device, mesh=mesh, in_specs=in_specs, out_specs=out_specs, check_vma=False
    )
```

```python
import functools

import jax
import jax.numpy as jnp
from jax import lax
from jax.experimental import pallas as pl
from jax.experimental.pallas import tpu as pltpu
from jax.sharding import PartitionSpec as P

MESH = pl.DeviceIdType.MESH
NB = 256
SIDE = 4
ZS = 8
ROWS, COLS = 768, 3072
WIDTHS = (768, 768, 768, 768)
STARTS = tuple(sum(WIDTHS[:c]) for c in range(len(WIDTHS)))
CHUNKS = range(len(WIDTHS))
S_WIDTHS = (768, 768, 768, 768)
S_STARTS = tuple(sum(S_WIDTHS[:c]) for c in range(len(S_WIDTHS)))
S_CHUNKS = range(len(S_WIDTHS))
TREE = (
    (1, 0, 0, 1), (1, 1, 1, 2), (1, 3, 3, 2), (2, 0, 0, 2), (0, 1, 2, 3), (0, 3, 2, 3), (1, 2, 3, 3), (2, 1, 1, 3),
    (2, 3, 0, 3), (3, 0, 0, 3), (0, 2, 2, 4), (2, 2, 1, 4), (3, 1, 0, 4), (3, 3, 0, 4), (3, 2, 0, 5),
)
DEPTH = 5
STEP_X, STEP_Y = (1, 0, -1, 0), (0, 1, 0, -1)
HALF = NB // 2
PLAN = (
    "picks0", "v1", "picks1", "z1", "es", "core0", "picks2", "v2", "core1", "picks3", "places", "z2", "ers", "n.SE",
    "major0", "core2", "v3", "major1", "core3", "minor0", "n.T0", "et", "z3", "major2", "ert", "n.TE", "v4", "m.SE",
    "minor1", "major3", "m.T0", "minor2", "z4", "m.TE", "n.T1", "n.T2", "p.SE", "v5", "c.S0", "p.T0", "p.TE",
    "minor3", "n.T3", "m.T1", "m.T2", "z5", "c.SE", "c.TE", "c.T0", "g.SE", "g.S0", "v6", "c.S1", "p.T1", "m.T3",
    "g.TE", "lowtop", "g.T0", "uppers0", "p.T2", "z6", "lowers", "c.T1", "p.T3", "g.S1", "v7", "c.S2", "update0",
    "c.T2", "g.T1", "uppers1", "g.S2", "c.T3", "update1", "g.T2", "v8", "c.S3", "uppers2", "g.T3", "update2",
    "uppers3", "g.S3", "update3",
)
BIG = SIDE * 16
SHARD = 16
BF = jnp.bfloat16
F32 = jnp.float32


def dot(a, b):
    return jnp.dot(a, b, preferred_element_type=F32)


def turned(row):
    n = row.shape[1]
    i = lax.broadcasted_iota(jnp.int32, (n, n), 0)
    j = lax.broadcasted_iota(jnp.int32, (n, n), 1)
    return jnp.sum(jnp.where(i == j, row, 0), axis=1, keepdims=True)


def kernel(
    a_hbm, piv_hbm, li_hbm, ui_hbm, ap,
    a, t, su, ps, po, xr, r1, q, r2, w, dl, oh, keep, se, l0t, u0w, li, ui, piv_ref,
    load_sem, part_sem,
    x_ss, x_rs, r1_ss, r1_rs, r2_ss, r2_rs, v_ss, v_rs,
    g1_ss, g1_rs, g2_ss, g2_rs, c_ss, c_rs, z_ss, z_rs, e_ss, e_rs, q_ss, q_rs,
):
    row = lax.axis_index("row")
    z = lax.axis_index("col")
    core = lax.rem(row, 2)
    yy = lax.rem(row // 2, SIDE)
    xx = row // (2 * SIDE)
    m = jnp.where(core == 0, xx, yy)
    n = jnp.where(core == 0, yy, xx)

    def at(mm, nn):
        mm, nn = lax.rem(mm + SIDE, SIDE), lax.rem(nn + SIDE, SIDE)
        return (jnp.where(core == 0, mm * SIDE + nn, nn * SIDE + mm) * 2 + core, z)

    sibling = (row + 1 - 2 * core, z)

    def along(k):
        return (row, lax.rem(z + k + ZS, ZS))

    s = su.at[pl.ds(0, 2 * NB)]

    def send(src, dst, ss_, rs_, dev):
        return pltpu.make_async_remote_copy(
            src_ref=src, dst_ref=dst, send_sem=ss_, recv_sem=rs_, device_id=dev, device_id_type=MESH
        )

    def load_a(c):
        cc = pl.ds(STARTS[c], WIDTHS[c])
        return pltpu.make_async_copy(a_hbm.at[:, cc], a.at[:, cc], part_sem.at[c])

    load_l = pltpu.make_async_copy(li_hbm, li, load_sem.at[1])
    load_u = pltpu.make_async_copy(ui_hbm, ui, load_sem.at[2])
    load_p = pltpu.make_async_copy(piv_hbm, piv_ref, load_sem.at[3])
    load_p.start()
    for c in CHUNKS:
        load_a(c).start()
    load_l.start()
    load_u.start()

    barrier = pltpu.get_barrier_semaphore()
    partners = [sibling]
    partners += [at(m + k, n) for k in (1, 2, 3)]
    partners += [at(m, n + k) for k in (1, 2, 3)]
    partners += [along(k) for k in range(1, ZS)]
    for dev in partners:
        pl.semaphore_signal(barrier, inc=1, device_id=dev, device_id_type=MESH)

    root = (m == 0) & (n == 0)
    off_lines = (m != 0) & (n != 0)

    @pl.when(root)
    def _():
        for mm in range(1, SIDE):
            for nn in range(1, SIDE):
                pl.semaphore_signal(barrier, inc=1, device_id=at(mm, nn), device_id_type=MESH)

    @pl.when(off_lines)
    def _():
        pl.semaphore_signal(barrier, inc=1, device_id=at(0, 0), device_id_type=MESH)

    more = jnp.where(root, (SIDE - 1) * (SIDE - 1), 0) + jnp.where(off_lines, 1, 0)
    pl.semaphore_wait(barrier, len(partners) + more)

    mine = core * NB

    def z_copy(blk, b, to, way, first):
        rows = pl.ds(b * NB, NB)
        cols = pl.ds(blk * NB, NB)
        src = a_hbm.at[rows, pl.ds(0, NB)] if first else w.at[rows, cols]
        return send(src, w.at[rows, cols], z_ss.at[blk, b, way], z_rs.at[blk, b], along(to))

    def own_panel(blk):
        return pltpu.make_async_copy(a_hbm.at[:, pl.ds(0, NB)], w.at[:, pl.ds(blk * NB, NB)], load_sem.at[4])

    def z_start(blk):
        @pl.when(z == blk)
        def _():
            for b in range(ROWS // NB):
                z_copy(blk, b, 1, 0, True).start()
                z_copy(blk, b, -1, 1, True).start()
            own_panel(blk).start()

    def z_wave(wave):
        for blk in (1, 0):
            rel = lax.rem(z - blk + ZS, ZS)
            for b in range(ROWS // NB):
                hops = wave - b
                if 1 <= hops <= 3:

                    @pl.when(rel == hops)
                    def _():
                        z_copy(blk, b, 1, 0, False).wait_recv()
                        z_copy(blk, b, 1, 0, False).start()

                if 1 <= hops <= 2:

                    @pl.when(rel == ZS - hops)
                    def _():
                        z_copy(blk, b, 1, 0, False).wait_recv()
                        z_copy(blk, b, -1, 1, False).start()

    def z_last(blk):
        rel = lax.rem(z - blk + ZS, ZS)

        @pl.when((rel == 4) | (rel == 5))
        def _():
            for b in range(ROWS // NB):
                z_copy(blk, b, 1, 0, False).wait_recv()

    def z_end(blk):
        rel = lax.rem(z - blk + ZS, ZS)

        for b in range(ROWS // NB):

            @pl.when(rel <= 3)
            def _():
                z_copy(blk, b, 1, 0, False).wait_send()

            @pl.when((rel == 0) | (rel >= 6))
            def _():
                z_copy(blk, b, -1, 1, False).wait_send()

    root = (m == 0) & (n == 0)

    def shard(mm, nn):
        return pl.ds(pl.multiple_of(mine + mm * BIG + nn * SHARD, SHARD), SHARD)

    own_rows = pltpu.make_async_copy(
        a_hbm.at[pl.ds(0, NB)], su.at[pl.ds(pl.multiple_of(mine, NB), NB), pl.ds(0, COLS)], load_sem.at[5]
    )
    flip = 1 - 2 * core

    depths, passes, inner = [], [], []
    for sign in (1, -1):
        px = lax.rem(sign * m + SIDE, SIDE)
        py = lax.rem(sign * flip * n + SIDE, SIDE)
        depth = 0
        go = [False] * 4
        for x, y, way, h in TREE:
            depth = depth + jnp.where((px == x) & (py == y), h, 0)
            go[way] = go[way] | ((px == (x - STEP_X[way]) % SIDE) & (py == (y - STEP_Y[way]) % SIDE))
        depths.append(depth)
        inner.append(go[0] | go[1] | go[2] | go[3])
        passes.append(go)

    def v_copy(tree, b, way, first=False):
        sign = 1 - 2 * tree
        cols = pl.ds(S_STARTS[b], S_WIDTHS[b])
        dst = su.at[pl.ds(pl.multiple_of(mine + tree * HALF, HALF), HALF), cols]
        src = a_hbm.at[pl.ds(tree * HALF, HALF), cols] if first else dst
        to = at(m + sign * STEP_X[way], n + sign * flip * STEP_Y[way])
        return send(src, dst, v_ss.at[tree, b, way], v_rs.at[tree, b], to)

    def s_start():
        @pl.when(root)
        def _():
            own_rows.start()
            for b in S_CHUNKS:
                for tree in range(2):
                    v_copy(tree, b, 0, True).start()

    def s_wave(wave):
        for b in S_CHUNKS:
            hops = wave - b
            if not 1 <= hops <= DEPTH:
                continue
            for tree in range(2):

                @pl.when((depths[tree] == hops) & inner[tree])
                def _():
                    v_copy(tree, b, 0).wait_recv()
                    for way in range(4):
                        if any(h == hops + 1 and e == way for _, _, e, h in TREE):

                            @pl.when(passes[tree][way])
                            def _():
                                v_copy(tree, b, way).start()

        if wave == 1:

            @pl.when(root)
            def _():
                own_rows.wait()

    def s_leaf(b):
        for tree in range(2):

            @pl.when(jnp.logical_not(inner[tree]))
            def _():
                v_copy(tree, b, 0).wait_recv()

    def s_end():
        for tree in range(2):
            for b in S_CHUNKS:
                for way in range(4):

                    @pl.when(passes[tree][way])
                    def _():
                        v_copy(tree, b, way).wait_send()

    bufs = (t, s)

    def q_copy(i):
        mm, nn = (i + 1) // SIDE, (i + 1) % SIDE
        rows = pl.ds(mm * BIG + nn * SHARD, SHARD)
        return send(a_hbm.at[rows, pl.ds(0, NB)], se, q_ss.at[i], q_rs, at(mm, nn))

    own_shard = pltpu.make_async_copy(a_hbm.at[pl.ds(0, SHARD), pl.ds(0, NB)], se, load_sem.at[6])

    def q_start():
        @pl.when(root & (z < 2))
        def _():
            for i in range(SIDE * SIDE - 1):
                q_copy(i).start()
            own_shard.start()

    def q_wait():
        @pl.when(jnp.logical_not(root) & (z < 2))
        def _():
            q_copy(0).wait_recv()

        @pl.when(root & (z < 2))
        def _():
            own_shard.wait()

    def q_end():
        @pl.when(root & (z < 2))
        def _():
            for i in range(SIDE * SIDE - 1):
                q_copy(i).wait_send()

    def e_copy(kind, blk, k):
        rows = shard(m, n)
        buf = bufs[kind]
        to = COLS + blk * NB if kind else COLS
        src = se if kind else buf.at[rows, pl.ds(0, NB)]
        return send(
            src, buf.at[rows, pl.ds(to, NB)], e_ss.at[kind, k - 1], e_rs.at[kind, blk], along(k)
        )

    def e_sources(kind):
        return ((0, z == 0), (1, z == 1)) if kind else ((0, z == 1 - core),)

    def e_start(kind):
        if kind:
            q_wait()
        for blk, here in e_sources(kind):

            @pl.when(here)
            def _():
                for k in (4, 3, 5, 2, 6, 1, 7):
                    e_copy(kind, blk, k).start()
                to = COLS + blk * NB if kind else COLS
                bufs[kind][shard(m, n), to : to + NB] = se[...] if kind else t[shard(m, n), 0:NB]

    def e_recv(kind):
        for blk, here in e_sources(kind):

            @pl.when(jnp.logical_not(here))
            def _():
                e_copy(kind, blk, 1).wait_recv()

    def e_end(kind):
        for blk, here in e_sources(kind):

            @pl.when(here)
            def _():
                for k in range(1, ZS):
                    e_copy(kind, blk, k).wait_send()

    def cols_of(c):
        return pl.ds(STARTS[c], WIDTHS[c])

    def x_copy(c):
        return send(ps.at[:, cols_of(c)], xr.at[:, cols_of(c)], x_ss.at[c], x_rs.at[c], sibling)

    def picks(c):
        load_a(c).wait()

        def body(i, carry):
            cc = pl.ds(pl.multiple_of(STARTS[c] + i * NB, NB), NB)
            both = dot(oh[...], a[:, cc]).astype(BF)
            ps[:, cc] = both[0:NB]
            po[:, cc] = both[NB : 2 * NB]
            return carry

        lax.fori_loop(0, WIDTHS[c] // NB, body, 0)
        x_copy(c).start()

    def r1_copy(c, k):
        g = lax.rem(m + k, SIDE)
        return send(
            po.at[pl.ds(pl.multiple_of(g * BIG, BIG), BIG), cols_of(c)], r1.at[k - 1, :, cols_of(c)],
            r1_ss.at[c, k - 1], r1_rs.at[c, k - 1], at(m + k, n),
        )

    def reduce_core(c):
        x_copy(c).wait_recv()
        po[:, cols_of(c)] = po[:, cols_of(c)] + xr[:, cols_of(c)]
        for k in (2, 1, 3):
            r1_copy(c, k).start()

    def r2_copy(c, k):
        g = lax.rem(n + k, SIDE)
        return send(
            q.at[pl.ds(pl.multiple_of(g * SHARD, SHARD), SHARD), cols_of(c)], r2.at[k - 1, :, cols_of(c)],
            r2_ss.at[c, k - 1], r2_rs.at[c, k - 1], at(m, n + k),
        )

    def reduce_major(c):
        for k in (1, 3, 2):
            r1_copy(c, k).wait_recv()
        cc = cols_of(c)
        own = po[pl.ds(pl.multiple_of(m * BIG, BIG), BIG), cc]
        q[:, cc] = (own + r1[0, :, cc]) + (r1[1, :, cc] + r1[2, :, cc])
        for k in (2, 1, 3):
            r2_copy(c, k).start()

    def reduce_minor(c):
        for k in (1, 3, 2):
            r2_copy(c, k).wait_recv()
        cc = cols_of(c)
        own = q[pl.ds(pl.multiple_of(n * SHARD, SHARD), SHARD), cc]
        t[shard(m, n), cc] = (own + r2[0, :, cc]) + (r2[1, :, cc] + r2[2, :, cc])

    items = [(1, S_STARTS[c], S_WIDTHS[c]) for c in S_CHUNKS] + [(1, COLS, 2 * NB), (0, COLS, NB)]
    items += [(0, STARTS[c], WIDTHS[c]) for c in CHUNKS]

    def g1_copy(i, k):
        kind, c0, width = items[i]
        part = bufs[kind].at[shard(m, n), pl.ds(c0, width)]
        return send(part, part, g1_ss.at[i, k - 1], g1_rs.at[i, k - 1], at(m, n + k))

    def gather_minor(i):
        for k in (2, 1, 3):
            g1_copy(i, k).start()

    def block(mm):
        return pl.ds(pl.multiple_of(mine + lax.rem(mm + SIDE, SIDE) * BIG, BIG), BIG)

    ways = ((0, 0, 1), (0, 1, -1), (0, 1, 1), (0, 0, -1), (-1, 0, 1), (1, 1, -1))

    def g2_copy(i, j):
        kind, c0, width = items[i]
        who, half, way = ways[j]
        part = bufs[kind].at[block(m + who), pl.ds(c0 + half * (width // 2), width // 2)]
        return send(part, part, g2_ss.at[i, j], g2_rs.at[i, j], at(m + way, n))

    def gather_major(i):
        for k in (1, 3, 2):
            g1_copy(i, k).wait_recv()
        for j in range(4):
            g2_copy(i, j).start()

    def gather_pass(i):
        g2_copy(i, 0).wait_recv()
        g2_copy(i, 4).start()
        g2_copy(i, 1).wait_recv()
        g2_copy(i, 5).start()

    def c_copy(i):
        kind, c0, width = items[i]
        part = bufs[kind].at[pl.ds(pl.multiple_of(mine, NB), NB), pl.ds(c0, width)]
        return send(part, part, c_ss.at[i], c_rs.at[i], sibling)

    def gather_core(i):
        if i < len(S_WIDTHS):
            s_leaf(i)
        else:
            for j in (2, 3, 4, 5):
                g2_copy(i, j).wait_recv()
        c_copy(i).start()

    def gathered(i):
        c_copy(i).wait_recv()

    def lowtop():
        load_l.wait()
        load_u.wait()
        l0t[...] = dot(t[NB : 2 * NB, COLS : COLS + NB], ui[0]).astype(BF)
        u0w[...] = dot(li[0], t[0:NB, COLS : COLS + NB]).astype(BF)

    def lowers():
        for blk in range(2):
            z_last(blk)

            @pl.when(z == blk)
            def _():
                own_panel(blk).wait()

        def body(b, carry):
            rows = pl.ds(pl.multiple_of(b * NB, NB), NB)
            stay = jnp.concatenate([keep[rows, :], keep[rows, :]], axis=1) > 0.5
            take = dl[rows, 0 : 2 * NB]
            w0 = jnp.where(stay, w[rows, 0:NB].astype(F32), dot(take, s[:, COLS : COLS + NB])).astype(BF)
            w1 = jnp.where(stay, w[rows, NB : 2 * NB].astype(F32), dot(take, s[:, COLS + NB : COLS + 2 * NB]))
            low0 = dot(w0, ui[0]).astype(BF)
            x1 = (w1 - dot(low0, u0w[...])).astype(BF)
            dl[rows, 2 * NB : 3 * NB] = -low0
            dl[rows, 3 * NB : 4 * NB] = -dot(x1, ui[1]).astype(BF)
            return carry

        lax.fori_loop(0, ROWS // NB, body, 0)

    def uppers(c):
        cc = cols_of(c)
        u0 = dot(li[0], t[0:NB, cc]).astype(BF)
        su[2 * NB : 3 * NB, cc] = u0
        x1 = (t[NB : 2 * NB, cc].astype(F32) - dot(l0t[...], u0)).astype(BF)
        su[3 * NB : 4 * NB, cc] = dot(li[1], x1).astype(BF)

    def update(c):
        def body(i, carry):
            cc = pl.ds(pl.multiple_of(S_STARTS[c] + i * NB, NB), NB)
            stay = jnp.concatenate([keep[...], keep[...]], axis=1) > 0.5
            base = jnp.where(stay, a[:, cc].astype(F32), 0.0)
            ap[:, cc] = (base + dot(dl[...], su[:, cc])).astype(BF)
            return carry

        lax.fori_loop(0, S_WIDTHS[c] // NB, body, 0)
        cc = pl.ds(S_STARTS[c], S_WIDTHS[c])

        @pl.when(row == 0)
        def _():
            ap[0:NB, cc] = su[2 * NB : 3 * NB, cc]

        @pl.when(row == 1)
        def _():
            ap[0:NB, cc] = su[3 * NB : 4 * NB, cc]

        if c == 0:
            panel_out()

    def panel_out():
        @pl.when((z == 0) & (row > 0))
        def _():
            ap[0:NB, 0:NB] = -dl[0:NB, 2 * NB : 3 * NB]

        @pl.when((z == 1) & (row > 1))
        def _():
            ap[0:NB, 0:NB] = -dl[0:NB, 3 * NB : 4 * NB]

        @pl.when(z == 0)
        def _():
            ap[NB:ROWS, 0:NB] = -dl[NB:ROWS, 2 * NB : 3 * NB]

        @pl.when(z == 1)
        def _():
            ap[NB:ROWS, 0:NB] = -dl[NB:ROWS, 3 * NB : 4 * NB]

        @pl.when((z == 0) & (row == 0))
        def _():
            ap[0:NB, 0:NB] = t[0:NB, 0:NB]

        @pl.when((z == 0) & (row == 1))
        def _():
            ap[0:NB, 0:NB] = l0t[...]

        @pl.when((z == 1) & (row == 1))
        def _():
            ap[0:NB, 0:NB] = (t[NB : 2 * NB, 0:NB].astype(F32) - dot(l0t[...], u0w[...])).astype(BF)

    q_start()
    s_start()
    z_start(0)
    z_start(1)

    load_p.wait()
    p0r, p1r = piv_ref[0:1, :], piv_ref[1:2, :]
    p0c, p1c = turned(p0r), turned(p1r)
    i0 = lax.broadcasted_iota(jnp.int32, (NB, NB), 0)
    i1 = lax.broadcasted_iota(jnp.int32, (NB, NB), 1)
    hit = p1c == p0r
    src1 = jnp.where(
        jnp.max(hit.astype(jnp.int32), axis=1, keepdims=True) > 0,
        jnp.sum(jnp.where(hit, i1, 0), axis=1, keepdims=True),
        p1c,
    )
    src_other = jnp.where(core == 0, src1, p0c)
    src_mine = jnp.where(core == 0, p0c, src1)
    for b in range(ROWS // NB):
        glob_r = b * (NB * 2 * SIDE * SIDE) + row * NB + i1
        oh[0:NB, b * NB : (b + 1) * NB] = (src_other == glob_r).astype(F32).astype(BF)
        oh[NB : 2 * NB, b * NB : (b + 1) * NB] = (src_mine == glob_r).astype(F32).astype(BF)

    def places():
        hit_top = p0r == NB + i0
        out_in = jnp.sum(jnp.where(hit_top, p1c, 0), axis=0, keepdims=True)
        met = jnp.max(hit.astype(jnp.int32), axis=0, keepdims=True) > 0
        met_at = jnp.sum(jnp.where(hit, NB + i0, 0), axis=0, keepdims=True)
        dest0 = jnp.where(p0r < NB, p0r, jnp.where(p0r < 2 * NB, out_in, jnp.where(met, met_at, p0r)))
        back = p0c == NB + i1
        dest1 = jnp.where(
            jnp.max(back.astype(jnp.int32), axis=0, keepdims=True) > 0,
            jnp.sum(jnp.where(back, i0, 0), axis=0, keepdims=True),
            p1r,
        )
        for b in range(ROWS // NB):
            rows = pl.ds(b * NB, NB)
            glob_c = b * (NB * 2 * SIDE * SIDE) + row * NB + i0
            d0 = dest0 == glob_c
            d1 = dest1 == glob_c
            dl[rows, 0:NB] = d0.astype(F32).astype(BF)
            dl[rows, NB : 2 * NB] = d1.astype(F32).astype(BF)
            moved = jnp.max(jnp.maximum(d0.astype(F32), d1.astype(F32)), axis=1, keepdims=True)
            keep[rows, :] = jnp.broadcast_to(1.0 - moved, (NB, 128))

    names = ["S%d" % c for c in S_CHUNKS] + ["SE", "TE"] + ["T%d" % c for c in CHUNKS]
    gathers = {"n": gather_minor, "m": gather_major, "p": gather_pass, "c": gather_core, "g": gathered}
    stages = {
        "picks": picks, "core": reduce_core, "major": reduce_major, "minor": reduce_minor,
        "uppers": uppers, "update": update, "z": z_wave, "v": s_wave,
    }
    single = {
        "et": (e_start, 0), "es": (e_start, 1), "ert": (e_recv, 0), "ers": (e_recv, 1),
        "lowers": (lowers,), "lowtop": (lowtop,), "places": (places,),
    }
    steps = []
    for word in PLAN:
        if "." in word:
            steps.append((gathers[word[0]], names.index(word[2:])))
        elif word in single:
            steps.append(single[word])
        else:
            steps.append((stages[word[:-1]], int(word[-1])))
    for step, *which in steps:
        step(*which)

    q_end()
    s_end()
    z_end(0)
    z_end(1)
    e_end(0)
    e_end(1)
    for c in CHUNKS:
        x_copy(c).wait_send()
        for k in (1, 2, 3):
            r1_copy(c, k).wait_send()
            r2_copy(c, k).wait_send()
    for i in range(len(items)):
        c_copy(i).wait_send()
    for i in range(len(S_WIDTHS), len(items)):
        for k in (1, 2, 3):
            g1_copy(i, k).wait_send()
        for j in range(6):
            g2_copy(i, j).wait_send()


def per_device(a_stored, pivots, l_inverse, u_inverse):
    chunks = len(WIDTHS)
    n_items = 2 + chunks + len(S_WIDTHS)
    dma = pltpu.SemaphoreType.DMA
    hbm = pl.BlockSpec(memory_space=pltpu.HBM)
    scratch = [
        pltpu.VMEM((ROWS, COLS), BF),
        pltpu.VMEM((2 * NB, COLS + NB), BF),
        pltpu.VMEM((4 * NB, COLS + 2 * NB), BF),
        pltpu.VMEM((NB, COLS), BF),
        pltpu.VMEM((NB, COLS), BF),
        pltpu.VMEM((NB, COLS), BF),
        pltpu.VMEM((3, BIG, COLS), BF),
        pltpu.VMEM((BIG, COLS), BF),
        pltpu.VMEM((3, SHARD, COLS), BF),
        pltpu.VMEM((ROWS, 2 * NB), BF),
        pltpu.VMEM((ROWS, 4 * NB), BF),
        pltpu.VMEM((2 * NB, ROWS), BF),
        pltpu.VMEM((ROWS, 128), F32),
        pltpu.VMEM((SHARD, NB), BF),
        pltpu.VMEM((NB, NB), BF),
        pltpu.VMEM((NB, NB), BF),
        pltpu.VMEM((2, NB, NB), BF),
        pltpu.VMEM((2, NB, NB), BF),
        pltpu.VMEM((2, NB), jnp.int32),
        dma((7,)), dma((chunks,)),
        dma((chunks,)), dma((chunks,)),
        dma((chunks, 3)), dma((chunks, 3)),
        dma((chunks, 3)), dma((chunks, 3)),
        dma((2, len(S_WIDTHS), 4)), dma((2, len(S_WIDTHS))),
        dma((n_items, 3)), dma((n_items, 3)),
        dma((n_items, 6)), dma((n_items, 6)),
        dma((n_items,)), dma((n_items,)),
        dma((2, 3, 2)), dma((2, 3)),
        dma((2, ZS - 1)), dma((2, 2)),
        dma((SIDE * SIDE - 1,)), dma,
    ]
    small = [pltpu.with_memory_space_constraint(v, pltpu.HBM) for v in (pivots, l_inverse, u_inverse)]
    return pl.pallas_call(
        kernel,
        out_shape=jax.ShapeDtypeStruct((ROWS, COLS), BF),
        in_specs=[hbm] * 4,
        out_specs=pl.BlockSpec(memory_space=pltpu.VMEM),
        scratch_shapes=scratch,
        compiler_params=pltpu.CompilerParams(
            collective_id=0, has_side_effects=True, vmem_limit_bytes=48 * 2**20
        ),
        name="panels",
    )(a_stored, *small)


def solution(mesh):
    in_specs = (P("row", "col"), P(), P(), P())
    out_specs = P("row", "col")
    return jax.shard_map(
        per_device, mesh=mesh, in_specs=in_specs, out_specs=out_specs, check_vma=False
    )
```
